128 devices in a mesh: ctx: 32 (over y, x, core), head: 4 (over z).
Axes of the slice: x: 4, y: 4, z: 4, core: 2. Of those that a mesh axis runs over, the one named last changes fastest.
Arguments:
- queries: bfloat16 [16384, 4096], P('ctx', 'head'), may hold values from -6 to 6
- keys: bfloat16 [16384, 1024], P('ctx', 'head'), may hold values from -6 to 6
- values: bfloat16 [16384, 1024], P('ctx', 'head'), may hold values from -6 to 6
- lengths: int32 [8], replicated, may hold values from 1 to 8192, 16384 in all
- out_weight: bfloat16 [4096, 8192], P('head'), may hold values from -0.125 to 0.125
Outputs:
- mixed: bfloat16 [16384, 8192], P('ctx', 'head')
The draws below stay inside these ranges and needn't reach their ends.
Inputs may be any that keep to these rules, and one draw needn't show every extreme that they name: Positive document lengths that sum to 16384; the longest is exactly 8192.
All inputs are finite; a program needn't handle non-finite values.
Results may differ from the reference program's by a relative error of at most 0.0065.
The reference program's roundings to bfloat16 on the way count: a program that leaves them out, or rounds other values in their place, can miss the bound.
Values may be sent and summed in bfloat16 or wider, within the bound.
A program may use at most 128 MiB of HBM per device.

```python
import math
import jax
import jax.numpy as jnp
import numpy as np
from jax import lax

D = 8192
QUERY_HEADS = 32
KEY_VALUE_HEADS = 8
HEAD_SIZE = 128
NDOCS = 8
TOKENS_PER_SHARD = 512
WINDOW_TOKENS = 16384
DOCMAX = 8192


def build_pair(key):
    key_q = jax.random.fold_in(key, 101)
    key_matrix = jax.random.fold_in(key, 202)
    queries = jnp.clip(2.5 * jax.random.normal(key_q, (WINDOW_TOKENS, QUERY_HEADS, HEAD_SIZE), jnp.float32), -6.0, 6.0)
    keys = jnp.clip(jax.random.normal(key_matrix, (WINDOW_TOKENS, KEY_VALUE_HEADS, HEAD_SIZE), jnp.float32), -6.0, 6.0)
    return (queries.reshape(WINDOW_TOKENS, QUERY_HEADS * HEAD_SIZE), keys.reshape(WINDOW_TOKENS, KEY_VALUE_HEADS * HEAD_SIZE))


def draw_queries(key, part):
    return build_pair(key)[0].astype(jnp.bfloat16)


def draw_keys(key, part):
    return build_pair(key)[1].astype(jnp.bfloat16)


def spiked(drawn, own_key, source, target, parts, factor):
    owner, partner = [(jnp.arange(drawn.shape[axis_at]) // (drawn.shape[axis_at] // parts)).reshape([-1 if axis == axis_at else 1 for axis in range(drawn.ndim)]) for axis_at in (source, target)]
    chosen = jax.random.permutation(own_key, parts)[partner]
    strong = (owner == chosen) | (owner == (partner + parts // 2) % parts)
    return jnp.where(strong, factor * drawn, drawn)


def levels(key, shape, split, low, largest):
    factor_of = 1.0
    for dim, parts in split:
        steps = jax.random.uniform(jax.random.fold_in(jax.random.fold_in(key, 6), dim), (parts,), jnp.float32, low / len(split), largest / len(split))
        factor_of = factor_of * jnp.repeat(jnp.exp(steps), shape[dim] // parts).reshape((-1,) + (1,) * (len(shape) - 1 - dim))
    return factor_of


def profile(number_of, total, limit, lean):
    weights = [(1 << 20) // math.isqrt(grade ** lean) + 1 for grade in range(2, number_of + 1)]
    rest, counts = total - limit - (number_of - 1), [1] * (number_of - 1)
    while rest > 0:
        candidates = [i for i in range(number_of - 1) if counts[i] < limit]
        pool, left = sum([weights[i] for i in candidates]), rest
        for i in candidates:
            extra = min(limit - counts[i], max(1, left * weights[i] // pool), rest)
            counts[i] = counts[i] + extra
            rest = rest - extra
    return np.array([limit] + counts)


def ragged(key, count, total, limit, slope):
    if count == 2:
        one = jax.random.randint(key, (), max(1, total - limit), min(limit, total - 1) + 1)
        return jnp.stack([one, total - one])
    sizes = jnp.asarray(profile(count, total, limit, slope), jnp.int32)
    twos = (count - 1) // 2
    giver, sink = sizes[1:1 + 2 * twos:2], sizes[2:2 + 2 * twos:2]
    slack = jnp.minimum(giver - 1, limit - sink)
    shifted = jax.random.randint(jax.random.fold_in(key, 1), (twos,), 0, 1 << 20) % (slack + 1)
    sizes = sizes.at[1:1 + 2 * twos:2].set(giver - shifted).at[2:2 + 2 * twos:2].set(sink + shifted)
    return sizes[jax.random.permutation(jax.random.fold_in(key, 2), count)]


def centred(rng, shape, scale, most, pieces=(), held_as=jnp.bfloat16):
    factor_of = levels(rng, shape, pieces, -0.22, 0.18) if pieces else 1.0
    drawn = jax.random.normal(rng, shape, jnp.float32) * scale * factor_of
    return jnp.minimum(jnp.maximum(drawn, -most), most).astype(held_as)


def gaussian_with(stream_key, shape, deviation, limit, cuts, heavy, kind=jnp.bfloat16):
    entries = deviation * jax.random.normal(stream_key, shape, jnp.float32)
    if cuts:
        entries = entries * levels(stream_key, shape, cuts, -0.22, 0.18)
    return jnp.clip(spiked(entries, jax.random.fold_in(stream_key, 3), *heavy), -limit, limit).astype(kind)


def setup_inputs(seed: int = 0) -> dict:
    splits = jax.random.split(jax.random.key(seed), 6)
    queries = draw_queries(jax.random.fold_in(splits[5], 71), 0)
    keys = draw_keys(jax.random.fold_in(splits[5], 71), 0)
    values = centred(splits[2], (WINDOW_TOKENS, KEY_VALUE_HEADS * HEAD_SIZE), 1.0, 6.0, ((0, 32), (1, 4)))
    lengths = ragged(splits[3], NDOCS, WINDOW_TOKENS, DOCMAX, 2).astype(jnp.int32)
    out_weight = gaussian_with(splits[4], (QUERY_HEADS * HEAD_SIZE, D), (QUERY_HEADS * HEAD_SIZE) ** -0.5, 0.125, ((0, 4),), (0, 1, 4, 2.0))
    return dict(queries=queries, keys=keys, values=values, lengths=lengths, out_weight=out_weight)


rope_base = 1000000.0
ramp_low = 23.0
ramp_high = 40.0
yarn_factor = 4.0
mscale = 0.1 * math.log(4.0) + 1.0

def doc_starts(positions, lengths):
    doc_ends = jnp.cumsum(lengths).astype(jnp.int32)
    picked = jnp.where(positions[:, None] >= doc_ends[None, :], lengths[None, :], 0)
    return lax.optimization_barrier(jnp.sum(picked, axis=1)).astype(jnp.int32)

def apply_rotary(heads, start_offsets):
    pair_index = jnp.arange(64).astype(jnp.float32)
    extrap = jnp.exp(-(2.0 * pair_index / 128.0) * math.log(rope_base))
    ramp = jnp.clip((pair_index - ramp_low) / (ramp_high - ramp_low), 0.0, 1.0)
    inverse = extrap / yarn_factor * ramp + extrap * (1.0 - ramp)
    angles = start_offsets.astype(jnp.float32)[:, None] * inverse[None, :]
    cosine = (jnp.cos(angles) * mscale)[:, None, :]
    sine = (jnp.sin(angles) * mscale)[:, None, :]
    first_half = heads[..., :64]
    second_half = heads[..., 64:]
    return jnp.concatenate([first_half * cosine - second_half * sine, second_half * cosine + first_half * sine], axis=-1)

def reference(queries, keys, values, lengths, out_weight):
    positions = jnp.arange(WINDOW_TOKENS).astype(jnp.int32)
    starts = doc_starts(positions, lengths)
    start_offsets = positions - starts
    query_group = QUERY_HEADS // KEY_VALUE_HEADS
    query_rotated = apply_rotary(queries.astype(jnp.float32).reshape(WINDOW_TOKENS, QUERY_HEADS, HEAD_SIZE), start_offsets).astype(jnp.bfloat16)
    key_rotated = apply_rotary(keys.astype(jnp.float32).reshape(WINDOW_TOKENS, KEY_VALUE_HEADS, HEAD_SIZE), start_offsets).astype(jnp.bfloat16)
    value_rows = values.reshape(WINDOW_TOKENS, KEY_VALUE_HEADS, HEAD_SIZE)
    window = DOCMAX + TOKENS_PER_SHARD
    scale = 1.0 / math.sqrt(HEAD_SIZE)

    def one_block(index):
        query_first = (index * TOKENS_PER_SHARD).astype(jnp.int32)
        kfirst = jnp.clip(query_first - DOCMAX, 0, WINDOW_TOKENS - window).astype(jnp.int32)
        query_block = lax.dynamic_slice_in_dim(query_rotated, query_first, TOKENS_PER_SHARD, 0).reshape(TOKENS_PER_SHARD, KEY_VALUE_HEADS, query_group, HEAD_SIZE)
        kblock = lax.dynamic_slice_in_dim(key_rotated, kfirst, window, 0)
        vblock = lax.dynamic_slice_in_dim(value_rows, kfirst, window, 0)
        scores = jnp.einsum('qgha,kga->ghqk', query_block.astype(jnp.float32), kblock.astype(jnp.float32)) * scale
        qpos = query_first + jnp.arange(TOKENS_PER_SHARD).astype(jnp.int32)
        kpos = kfirst + jnp.arange(window).astype(jnp.int32)
        qstart = lax.dynamic_slice_in_dim(starts, query_first, TOKENS_PER_SHARD, 0)
        visible = (kpos[None, :] <= qpos[:, None]) & (kpos[None, :] >= qstart[:, None])
        scores = jnp.where(visible, scores, -1e+30)
        top = lax.optimization_barrier(jnp.max(scores, axis=-1))
        weights = jnp.where(visible, jnp.exp(scores - top[..., None]), 0.0)
        total = lax.optimization_barrier(jnp.sum(weights, axis=-1))
        summed = jnp.einsum('ghqk,kga->ghqa', weights.astype(jnp.bfloat16).astype(jnp.float32), vblock.astype(jnp.float32))
        attended = summed / total[..., None]
        return jnp.transpose(attended, (2, 0, 1, 3)).astype(jnp.bfloat16).reshape(TOKENS_PER_SHARD, QUERY_HEADS * HEAD_SIZE)
    blocks = lax.map(one_block, jnp.arange(WINDOW_TOKENS // TOKENS_PER_SHARD).astype(jnp.int32))
    attended = blocks.reshape(WINDOW_TOKENS, QUERY_HEADS * HEAD_SIZE)
    return jnp.dot(attended, out_weight, preferred_element_type=jnp.float32).astype(jnp.bfloat16)
```

```python
import functools
import math

import jax
import jax.numpy as jnp
from jax import lax
from jax.experimental import pallas as pl
from jax.experimental.pallas import tpu as pltpu
from jax.sharding import PartitionSpec as P

f32, bf16 = jnp.float32, jnp.bfloat16
rope_base = 1000000.0
ramp_low = 23.0
ramp_high = 40.0
yarn_factor = 4.0
mscale = 0.1 * math.log(4.0) + 1.0
neg_large = -1e30
exp2_scale = math.log2(math.e) / math.sqrt(128.0)
doc_penalty = 131072.0

NDOCS = 8
BLOCK = 1024
GROUP = 4
TILE = 1024


def doc_bounds(lengths):
    index = jnp.arange(NDOCS)
    ends = jnp.sum(jnp.where(index[None, :] <= index[:, None], lengths[None, :], 0), axis=1)
    return ends - lengths, ends


def doc_one_hot(positions, starts, ends):
    pad = 128 - NDOCS
    starts = jnp.pad(starts, (0, pad))[None, :]
    ends = jnp.pad(ends, (0, pad))[None, :]
    at = positions[:, None]
    return ((at >= starts) & (at < ends)).astype(f32)


def rotary_tables(start_offsets):
    pair_index = jnp.arange(64).astype(f32)
    extrap = jnp.exp(-(2.0 * pair_index / 128.0) * math.log(rope_base))
    ramp = jnp.clip((pair_index - ramp_low) / (ramp_high - ramp_low), 0.0, 1.0)
    inverse = extrap / yarn_factor * ramp + extrap * (1.0 - ramp)
    angles = start_offsets.astype(f32)[:, None] * inverse[None, :]
    return jnp.cos(angles) * mscale, jnp.sin(angles) * mscale


def rotate(heads, cosine, sine):
    cosine, sine = cosine[:, None, :], sine[:, None, :]
    first = heads[..., :64].astype(f32)
    second = heads[..., 64:].astype(f32)
    return jnp.concatenate(
        [first * cosine - second * sine, second * cosine + first * sine], axis=-1
    ).astype(bf16)


def attention_kernel(first_ref, q_ref, k_ref, v_ref, o_ref, top, total, acc):
    own = first_ref[1]

    def step(block, tile, diagonal):
        cols = pl.ds(pl.multiple_of(tile * TILE, TILE), TILE)
        keys = k_ref[pl.ds(pl.multiple_of(block * BLOCK, BLOCK), BLOCK), :]
        s = jnp.dot(keys, q_ref[:, cols], preferred_element_type=f32)
        if diagonal:
            at = lax.broadcasted_iota(jnp.int32, s.shape, 0)
            query = lax.broadcasted_iota(jnp.int32, s.shape, 1)
            s = jnp.where(at <= query, s, neg_large)
            new = jnp.max(s, axis=0, keepdims=True)
        else:
            old = top[:, cols]
            new = jnp.maximum(old, jnp.max(s, axis=0, keepdims=True))
        p = jnp.exp2((s - new) * exp2_scale)
        if diagonal:
            total[:, cols] = jnp.sum(p, axis=0, keepdims=True)
        else:
            scale = jnp.exp2((old - new) * exp2_scale)
            total[:, cols] = total[:, cols] * scale + jnp.sum(p, axis=0, keepdims=True)
        top[:, cols] = new
        values = v_ref[pl.ds(pl.multiple_of(block * 128, 128), 128), :]
        summed = jnp.dot(values, p.astype(bf16), preferred_element_type=f32)
        acc[:, cols] = summed if diagonal else acc[:, cols] * scale + summed

    def diagonal_tile(tile, _):
        step(own, tile, True)
        return 0

    lax.fori_loop(0, GROUP * BLOCK // TILE, diagonal_tile, 0)

    def one_block(block, _):
        def one_tile(tile, _):
            step(block, tile, False)
            return 0

        return lax.fori_loop(0, GROUP * BLOCK // TILE, one_tile, 0)

    lax.fori_loop(first_ref[0], own, one_block, 0)
    o_ref[...] = (acc[...] / total[...]).astype(bf16)


def attention(first, q, k, v):
    vmem = pl.BlockSpec(memory_space=pltpu.VMEM)
    columns = q.shape[1]
    return pl.pallas_call(
        attention_kernel,
        out_shape=jax.ShapeDtypeStruct((128, columns), bf16),
        in_specs=[pl.BlockSpec(memory_space=pltpu.SMEM), vmem, vmem, vmem],
        out_specs=vmem,
        scratch_shapes=[
            pltpu.VMEM((1, columns), f32),
            pltpu.VMEM((1, columns), f32),
            pltpu.VMEM((128, columns), f32),
        ],
        compiler_params=pltpu.CompilerParams(vmem_limit_bytes=52 * 2**20),
    )(first, q, k, v)


def per_device(queries, keys, values, lengths, out_weight):
    device = lax.axis_index("ctx")
    z = lax.axis_index("head")
    core = device % 2
    chip = device // 2
    other = 1 - core
    swap = [(i, i ^ 1) for i in range(32)]
    parity = [[i for i in range(32) if i % 2 == c] for c in (0, 1)]

    def part(x, width, which):
        return lax.dynamic_slice_in_dim(x, which * width, width, 1)

    rows = lax.dynamic_slice_in_dim(out_weight, core * 512, 512, 0)
    weights = [part(rows, 2048, z)]
    for shift in (1, 2, 3):
        block = part(rows, 2048, (z + shift) % 4)
        weights.append(lax.ppermute(block, "head", [(i, (i + shift) % 4) for i in range(4)]))

    mine = jnp.concatenate([part(queries, 512, core), part(keys, 128, core), part(values, 128, core)], 1)
    theirs = jnp.concatenate([part(queries, 512, other), part(keys, 128, other), part(values, 128, other)], 1)
    came = lax.ppermute(theirs, "ctx", swap)
    both = jnp.where(core == 0, jnp.concatenate([mine, came], 0), jnp.concatenate([came, mine], 0))

    starts, ends = doc_bounds(lengths)
    positions = chip * BLOCK + jnp.arange(BLOCK)
    one_hot = doc_one_hot(positions, starts, ends)
    qstart = jnp.sum(jnp.where(positions[:, None] >= ends[None, :], lengths[None, :], 0), axis=1)
    cosine, sine = rotary_tables(positions - qstart)
    turned = rotate(both[:, :640].reshape(BLOCK, 5, 128), cosine, sine)
    q = jnp.transpose(turned[:, :4], (2, 1, 0)).reshape(128, GROUP * BLOCK)
    penalty = jnp.transpose((one_hot - 1.0) * doc_penalty).astype(bf16)
    q = jnp.concatenate([q, jnp.tile(penalty, (1, GROUP))], 0)
    k = lax.all_gather(turned[:, 4], "ctx", axis=0, tiled=True, axis_index_groups=parity)
    v = lax.all_gather(both[:, 640:].T, "ctx", axis=0, tiled=True, axis_index_groups=parity)
    hot = doc_one_hot(jnp.arange(16 * BLOCK), starts, ends).astype(bf16)
    k = jnp.concatenate([k, hot], 1)
    first = jnp.stack([qstart[0] // BLOCK, chip]).astype(jnp.int32)
    attended = attention(first, q, k, v)

    attended = jnp.transpose(attended.reshape(128, GROUP, BLOCK), (2, 1, 0)).reshape(BLOCK, 512)
    gathered = lax.all_gather(attended, "head", axis=0)
    partial = 0.0
    for shift in range(4):
        source = (z - shift + 4) % 4
        from_z = lax.dynamic_index_in_dim(gathered, source, 0, keepdims=False)
        partial = partial + jnp.dot(from_z, weights[shift], preferred_element_type=f32)
    kept = lax.dynamic_slice_in_dim(partial, core * 512, 512, 0)
    sent = lax.dynamic_slice_in_dim(partial, other * 512, 512, 0)
    return (kept + lax.ppermute(sent, "ctx", swap)).astype(bf16)


def solution(mesh):
    return jax.shard_map(
        per_device,
        mesh=mesh,
        in_specs=(P("ctx", "head"), P("ctx", "head"), P("ctx", "head"), P(), P("head", None)),
        out_specs=P("ctx", "head"),
        check_vma=False,
    )
```

```python
import math

import jax
import jax.numpy as jnp
from jax import lax
from jax.experimental import pallas as pl
from jax.experimental.pallas import tpu as pltpu
from jax.sharding import PartitionSpec as P

f32, bf16 = jnp.float32, jnp.bfloat16
rope_base = 1000000.0
ramp_low = 23.0
ramp_high = 40.0
yarn_factor = 4.0
mscale = 0.1 * math.log(4.0) + 1.0
neg_large = -1e30
exp2_scale = math.log2(math.e) / math.sqrt(128.0)
doc_penalty = 131072.0

NDOCS = 8
BLOCK = 1024
GROUP = 4
HALF = 512
CHUNK = 256
TILE = GROUP * CHUNK
CHUNKS = BLOCK // CHUNK
SLOTS = 9
OUTER = 6
MESH = pl.DeviceIdType.MESH


def doc_bounds(lengths):
    index = jnp.arange(NDOCS)
    ends = jnp.sum(jnp.where(index[None, :] <= index[:, None], lengths[None, :], 0), axis=1)
    return ends - lengths, ends


def inverse_frequencies():
    pair_index = jnp.arange(64).astype(f32)
    extrap = jnp.exp(-(2.0 * pair_index / 128.0) * math.log(rope_base))
    ramp = jnp.clip((pair_index - ramp_low) / (ramp_high - ramp_low), 0.0, 1.0)
    return extrap / yarn_factor * ramp + extrap * (1.0 - ramp)


def prepare_kernel(lengths, first_ref, inverse, queries, keys, values, q_ref, k_ref, v_ref):
    first = first_ref[0]
    lane = lax.broadcasted_iota(jnp.int32, (HALF, 128), 1)
    at = first + lax.broadcasted_iota(jnp.int32, (HALF, 128), 0)
    start = jnp.zeros((HALF, 128), jnp.int32)
    document = lax.broadcasted_iota(jnp.int32, (128, HALF), 0)
    across = first + lax.broadcasted_iota(jnp.int32, (128, HALF), 1)
    hidden = document < NDOCS
    end = 0
    for j in range(NDOCS):
        begin, end = end, end + lengths[j]
        start = start + jnp.where(at >= end, lengths[j], 0)
        hidden = hidden & ~((document == j) & (across >= begin) & (across < end))
    penalty = jnp.where(hidden, -doc_penalty, 0.0).astype(bf16)
    angles = (at - start).astype(f32) * inverse[...]
    cosine = jnp.cos(angles) * mscale
    sine = jnp.sin(angles) * mscale
    sine = jnp.where(lane < 64, -sine, sine)

    def rotated(ref, head):
        x = ref[:, head * 128 : (head + 1) * 128].astype(f32)
        return x * cosine + pltpu.roll(x, 64, 1) * sine

    for kv in range(2):
        for member in range(GROUP):
            turned = jnp.transpose(rotated(queries, kv * GROUP + member)).astype(bf16)
            for chunk in range(HALF // CHUNK):
                cols = slice(chunk * TILE + member * CHUNK, chunk * TILE + (member + 1) * CHUNK)
                tokens = slice(chunk * CHUNK, (chunk + 1) * CHUNK)
                q_ref[kv, 0:128, cols] = turned[:, tokens]
                q_ref[kv, 128:256, cols] = penalty[:, tokens]
        k_ref[kv] = rotated(keys, kv).astype(bf16)
        v_ref[kv] = jnp.transpose(values[:, kv * 128 : (kv + 1) * 128].astype(f32)).astype(bf16)


def prepare(lengths, first, queries, keys, values):
    inverse = inverse_frequencies()
    inverse = jnp.concatenate([inverse, inverse])[None, :]
    smem = pl.BlockSpec(memory_space=pltpu.SMEM)
    vmem = pl.BlockSpec(memory_space=pltpu.VMEM)
    return pl.pallas_call(
        prepare_kernel,
        out_shape=(
            jax.ShapeDtypeStruct((2, 256, GROUP * HALF), bf16),
            jax.ShapeDtypeStruct((2, HALF, 128), bf16),
            jax.ShapeDtypeStruct((2, 128, HALF), bf16),
        ),
        in_specs=[smem, smem, vmem, vmem, vmem, vmem],
        out_specs=(vmem, vmem, vmem),
        compiler_params=pltpu.CompilerParams(vmem_limit_bytes=40 * 2**20),
    )(lengths, first, inverse, queries, keys, values)


def main_kernel(
    bounds, qp, kp, vp, w_hbm, o_ref,
    q, kbuf, vbuf, top, total, acc, wbuf, att, given, taken,
    local_sem, swap_send, swap_recv, k_send, k_recv, v_send, v_recv,
    w_send, w_recv, c_send, c_recv, a_send, a_recv, p_send, p_recv,
):
    ctx = lax.axis_index("ctx")
    z = lax.axis_index("head")
    core = lax.rem(ctx, 2)
    chip = ctx // 2
    x = lax.rem(chip, 4)
    y = chip // 4
    other = 1 - core
    mate = (ctx + 1 - 2 * core, z)

    def at(x_, y_):
        return ((y_ * 4 + x_) * 2 + core, z)

    def remote(src, dst, send, recv, device):
        return pltpu.make_async_remote_copy(
            src_ref=src, dst_ref=dst, send_sem=send, recv_sem=recv, device_id=device, device_id_type=MESH
        )

    begin, end = bounds[0:1, :], bounds[1:2, :]
    for slot in range(SLOTS):
        where = (chip - slot) * BLOCK + lax.broadcasted_iota(jnp.int32, (BLOCK, 128), 0)
        kbuf[slot, :, 128:256] = jnp.where((where >= begin) & (where < end), 1.0, 0.0).astype(bf16)

    barrier = pltpu.get_barrier_semaphore()
    pl.semaphore_signal(barrier, inc=1, device_id=mate, device_id_type=MESH)
    for step in (1, 2, 3):
        for device in (
            at(lax.rem(x + step, 4), y),
            at(x, lax.rem(y + step, 4)),
            (ctx, lax.rem(z + step, 4)),
        ):
            pl.semaphore_signal(barrier, inc=1, device_id=device, device_id_type=MESH)
    pl.semaphore_wait(barrier, 10)

    mine = pl.ds(pl.multiple_of(core * HALF, HALF), HALF)
    mine_q = pl.ds(pl.multiple_of(core * GROUP * HALF, GROUP * HALF), GROUP * HALF)
    swaps = [
        remote(kp.at[other], kbuf.at[0, mine, pl.ds(0, 128)], swap_send.at[0], swap_recv.at[0], mate),
        remote(vp.at[other], vbuf.at[0, :, mine], swap_send.at[1], swap_recv.at[1], mate),
        remote(qp.at[other], q.at[:, mine_q], swap_send.at[2], swap_recv.at[2], mate),
    ]
    for copy in swaps:
        copy.start()
    rows = core * HALF

    def columns(s):
        return pl.ds(pl.multiple_of(lax.rem(z + s, 4) * 2048, 2048), 2048)

    piece = pl.ds(pl.multiple_of(y * 128, 128), 128)
    w_own = pltpu.make_async_copy(
        w_hbm.at[pl.ds(pl.multiple_of(rows, HALF), HALF), columns(0)], wbuf.at[0], local_sem.at[3]
    )
    w_piece = remote(
        w_hbm.at[pl.ds(pl.multiple_of(rows + y * 128, 128), 128), columns(2)],
        wbuf.at[2, piece, :], w_send.at[2], w_recv.at[2], (ctx, lax.rem(z + 2, 4)),
    )
    w_whole = [
        remote(
            w_hbm.at[pl.ds(pl.multiple_of(rows, HALF), HALF), columns(s)],
            wbuf.at[s], w_send.at[s], w_recv.at[s], (ctx, lax.rem(z + s, 4)),
        )
        for s in (1, 3)
    ]
    locals_ = [
        pltpu.make_async_copy(kp.at[core], kbuf.at[0, mine, pl.ds(0, 128)], local_sem.at[0]),
        pltpu.make_async_copy(vp.at[core], vbuf.at[0, :, mine], local_sem.at[1]),
        pltpu.make_async_copy(qp.at[core], q.at[:, mine_q], local_sem.at[2]),
    ]
    for copy in locals_:
        copy.start()
    w_piece.start()
    for copy in w_whole:
        copy.start()
    w_own.start()

    def share(slot, far, device, index):
        return (
            remote(kbuf.at[slot, :, pl.ds(0, 128)], kbuf.at[far, :, pl.ds(0, 128)], k_send.at[index], k_recv.at[far], device),
            remote(vbuf.at[slot], vbuf.at[far], v_send.at[index], v_recv.at[far], device),
        )

    down = [(y + s <= 3, share(0, 4 * s, at(x, lax.rem(y + s, 4)), s - 1)) for s in (1, 2)]
    row = []
    for s in (1, 2, 3):
        x_ = lax.rem(x + s, 4)
        row.append((x + s <= 3, share(0, s, at(x_, y), 1 + s)))
    second, third = [], []
    for s in (1, 2, 3):
        x_ = lax.rem(x + s, 4)
        second.append((y >= 1, share(4, 4 + x_ - x, at(x_, y), 4 + s)))
        third.append(((y >= 2) & (x_ < x), share(8, lax.rem(8 + x_ - x, 9), at(x_, y), 7 + s)))

    def go(list_):
        for condition, copies in list_:
            @pl.when(condition)
            def _():
                for copy in copies:
                    copy.start()

    def arrived(slot):
        for copy in share(slot, slot, mate, 0):
            copy.wait_recv()

    for copy in swaps[:2]:
        copy.wait_recv()
    for copy in locals_[:2]:
        copy.wait()
    go(down)
    go(row)
    swaps[2].wait_recv()
    locals_[2].wait()

    for chunk in range(CHUNKS):
        cols = slice(chunk * TILE, (chunk + 1) * TILE)
        seen = (chunk + 1) * CHUNK
        s = jnp.dot(kbuf[0, 0:seen, :], q[:, cols], preferred_element_type=f32)
        key = lax.broadcasted_iota(jnp.int32, s.shape, 0)
        query = chunk * CHUNK + lax.rem(lax.broadcasted_iota(jnp.int32, s.shape, 1), CHUNK)
        s = jnp.where(key <= query, s, neg_large)
        new = jnp.max(s, axis=0, keepdims=True)
        p = jnp.exp2((s - new) * exp2_scale)
        top[chunk] = new
        total[chunk] = jnp.sum(p, axis=0, keepdims=True)
        acc[chunk] = jnp.dot(vbuf[0, :, 0:seen], p.astype(bf16), preferred_element_type=f32)

    def add(slot, chunk):
        cols = pl.ds(pl.multiple_of(chunk * TILE, TILE), TILE)
        s = jnp.dot(kbuf[slot], q[:, cols], preferred_element_type=f32)
        old = top[chunk]
        new = jnp.maximum(old, jnp.max(s, axis=0, keepdims=True))
        p = jnp.exp2((s - new) * exp2_scale)
        scale = jnp.exp2((old - new) * exp2_scale)
        total[chunk] = total[chunk] * scale + jnp.sum(p, axis=0, keepdims=True)
        top[chunk] = new
        acc[chunk] = acc[chunk] * scale + jnp.dot(vbuf[slot], p.astype(bf16), preferred_element_type=f32)

    def slot_of(i):
        of_second = jnp.where(i < 4, i, i + 1)
        of_third = jnp.where(i == x + 4, 8, i)
        later = jnp.where(i == x, 4, jnp.where(i <= x + 3, of_second, of_third))
        return jnp.where(i < x, i + 1, later)

    def forward(slot, rows_before, list_):
        @pl.when(y >= rows_before)
        def _():
            arrived(slot)
        go(list_)

    c_copies = []
    for s in (1, 2, 3):
        y_ = lax.rem(y + s, 4)
        c_copies.append(
            remote(wbuf.at[2, piece, :], wbuf.at[2, piece, :], c_send.at[s - 1], c_recv.at[s - 1], at(x, y_))
        )

    def block_step(i, _):
        @pl.when(i == jnp.minimum(x, 1))
        def _():
            forward(4, 1, second)

        @pl.when(i == 3)
        def _():
            forward(8, 2, third)

        @pl.when(i == 4)
        def _():
            w_piece.wait_recv()
            for copy in c_copies:
                copy.start()

        slot = slot_of(i)

        @pl.when(chip >= slot)
        def _():
            @pl.when((slot != 4) & (slot != 8))
            def _():
                arrived(slot)

            def one(chunk, _):
                add(slot, chunk)
                return 0

            lax.fori_loop(0, CHUNKS, one, 0)

        return 0

    lax.fori_loop(0, OUTER, block_step, 0)
    for i in range(OUTER, 8):
        slot = slot_of(i)

        @pl.when((chip >= slot) & (slot != 4) & (slot != 8))
        def _():
            arrived(slot)

    def chunk_of(i):
        return lax.rem(i + 2 * other, CHUNKS)

    def sends(i):
        chunk = chunk_of(i)
        return [
            remote(att.at[i, 0], att.at[i, s], a_send.at[i, s], a_recv.at[i, s], (ctx, lax.rem(z + s, 4)))
            for s in (1, 2, 3)
        ]

    def finish(i, _):
        chunk = chunk_of(i)
        for j in range(OUTER, 8):
            slot = slot_of(j)

            @pl.when(chip >= slot)
            def _():
                add(slot, chunk)

        out = acc[chunk] / total[chunk]
        for member in range(GROUP):
            cols = slice(member * CHUNK, (member + 1) * CHUNK)
            att[i, 0, :, member * 128 : (member + 1) * 128] = jnp.transpose(out[:, cols]).astype(bf16)
        for copy in sends(i):
            copy.start()
        return 0

    lax.fori_loop(0, CHUNKS, finish, 0)

    w_own.wait()
    for copy in w_whole:
        copy.wait_recv()
    for s in (1, 2, 3):
        remote(
            wbuf.at[2, piece, :],
            wbuf.at[2, pl.ds(pl.multiple_of(lax.rem(y + 4 - s, 4) * 128, 128), 128), :],
            c_send.at[s - 1], c_recv.at[s - 1], mate,
        ).wait_recv()

    def exchange(i):
        return remote(given.at[i], taken.at[i], p_send.at[i], p_recv.at[i], mate)

    def project(i, keep):
        for copy in sends(i):
            copy.wait_recv()

        def some(n, _):
            cols = pl.ds(pl.multiple_of(n * 512, 512), 512)
            part = jnp.dot(att[i, 0], wbuf[0, :, cols], preferred_element_type=f32)
            for s in (1, 2, 3):
                part = part + jnp.dot(att[i, s], wbuf[s, :, cols], preferred_element_type=f32)
            keep(cols, part)
            return 0

        lax.fori_loop(0, 4, some, 0)

    for i in (0, 1):
        def give(cols, part):
            given[i, :, cols] = part

        project(i, give)
        exchange(i).start()
    for i in (0, 1):
        exchange(i).wait_recv()

        def keep(cols, part):
            o_ref[i * CHUNK : (i + 1) * CHUNK, cols] = (part + taken[i, :, cols]).astype(bf16)

        project(i + 2, keep)

    for copy in swaps + w_whole + [w_piece] + c_copies:
        copy.wait_send()
    for list_ in (down, row, second, third):
        for condition, copies in list_:
            @pl.when(condition)
            def _():
                for copy in copies:
                    copy.wait_send()
    for i in range(CHUNKS):
        for copy in sends(i):
            copy.wait_send()
    for i in (0, 1):
        exchange(i).wait_send()


def attend_and_project(bounds, q, k, v, out_weight):
    vmem = pl.BlockSpec(memory_space=pltpu.VMEM)
    dma = pltpu.SemaphoreType.DMA
    return pl.pallas_call(
        main_kernel,
        out_shape=jax.ShapeDtypeStruct((HALF, 2048), bf16),
        in_specs=[vmem, vmem, vmem, vmem, pl.BlockSpec(memory_space=pl.ANY)],
        out_specs=vmem,
        scratch_shapes=[
            pltpu.VMEM((256, GROUP * BLOCK), bf16),
            pltpu.VMEM((SLOTS, BLOCK, 256), bf16),
            pltpu.VMEM((SLOTS, 128, BLOCK), bf16),
            pltpu.VMEM((CHUNKS, 1, TILE), f32),
            pltpu.VMEM((CHUNKS, 1, TILE), f32),
            pltpu.VMEM((CHUNKS, 128, TILE), f32),
            pltpu.VMEM((4, HALF, 2048), bf16),
            pltpu.VMEM((CHUNKS, 4, CHUNK, 512), bf16),
            pltpu.VMEM((2, CHUNK, 2048), f32),
            pltpu.VMEM((2, CHUNK, 2048), f32),
            dma((4,)), dma((3,)), dma((3,)),
            dma((11,)), dma((SLOTS,)), dma((11,)), dma((SLOTS,)),
            dma((4,)), dma((4,)), dma((3,)), dma((3,)),
            dma((CHUNKS, 4)), dma((CHUNKS, 4)), dma((2,)), dma((2,)),
        ],
        compiler_params=pltpu.CompilerParams(
            collective_id=0, has_side_effects=True, vmem_limit_bytes=60 * 2**20
        ),
    )(bounds, q, k, v, out_weight)


def per_device(queries, keys, values, lengths, out_weight):
    device = lax.axis_index("ctx")
    starts, ends = doc_bounds(lengths)
    bounds = jnp.pad(jnp.stack([starts, ends]), ((0, 6), (0, 128 - NDOCS)))
    first = (device * HALF).astype(jnp.int32).reshape(1)
    q, k, v = prepare(lengths, first, queries, keys, values)
    return attend_and_project(bounds, q, k, v, out_weight)


def solution(mesh):
    return jax.shard_map(
        per_device,
        mesh=mesh,
        in_specs=(P("ctx", "head"), P("ctx", "head"), P("ctx", "head"), P(), P("head", None)),
        out_specs=P("ctx", "head"),
        check_vma=False,
    )
```

```python
import math

import jax
import jax.numpy as jnp
from jax import lax
from jax.experimental import pallas as pl
from jax.experimental.pallas import tpu as pltpu
from jax.sharding import PartitionSpec as P

f32, bf16 = jnp.float32, jnp.bfloat16
rope_base = 1000000.0
ramp_low = 23.0
ramp_high = 40.0
yarn_factor = 4.0
mscale = 0.1 * math.log(4.0) + 1.0
neg_large = -1e30
exp2_scale = math.log2(math.e) / math.sqrt(128.0)
doc_penalty = 131072.0

NDOCS = 8
BLOCK = 1024
GROUP = 4
HALF = 512
CHUNK = 256
TILE = GROUP * CHUNK
CHUNKS = BLOCK // CHUNK
SLOTS = 9
LAST = 4
MESH = pl.DeviceIdType.MESH


def doc_bounds(lengths):
    index = jnp.arange(NDOCS)
    ends = jnp.sum(jnp.where(index[None, :] <= index[:, None], lengths[None, :], 0), axis=1)
    return ends - lengths, ends


def inverse_frequencies():
    pair_index = jnp.arange(64).astype(f32)
    extrap = jnp.exp(-(2.0 * pair_index / 128.0) * math.log(rope_base))
    ramp = jnp.clip((pair_index - ramp_low) / (ramp_high - ramp_low), 0.0, 1.0)
    return extrap / yarn_factor * ramp + extrap * (1.0 - ramp)


def prepare_kernel(lengths, first_ref, inverse, queries, keys, values, q_ref, k_ref, v_ref):
    first = first_ref[0]
    lane = lax.broadcasted_iota(jnp.int32, (HALF, 128), 1)
    at = first + lax.broadcasted_iota(jnp.int32, (HALF, 128), 0)
    start = jnp.zeros((HALF, 128), jnp.int32)
    document = lax.broadcasted_iota(jnp.int32, (128, HALF), 0)
    across = first + lax.broadcasted_iota(jnp.int32, (128, HALF), 1)
    hidden = document < NDOCS
    end = 0
    for j in range(NDOCS):
        begin, end = end, end + lengths[j]
        start = start + jnp.where(at >= end, lengths[j], 0)
        hidden = hidden & ~((document == j) & (across >= begin) & (across < end))
    penalty = jnp.where(hidden, -doc_penalty, 0.0).astype(bf16)
    angles = (at - start).astype(f32) * inverse[...]
    cosine = jnp.cos(angles) * mscale
    sine = jnp.sin(angles) * mscale
    sine = jnp.where(lane < 64, -sine, sine)

    def rotated(ref, head):
        x = ref[:, head * 128 : (head + 1) * 128].astype(f32)
        return x * cosine + pltpu.roll(x, 64, 1) * sine

    for kv in range(2):
        for member in range(GROUP):
            turned = jnp.transpose(rotated(queries, kv * GROUP + member)).astype(bf16)
            for chunk in range(HALF // CHUNK):
                cols = slice(chunk * TILE + member * CHUNK, chunk * TILE + (member + 1) * CHUNK)
                tokens = slice(chunk * CHUNK, (chunk + 1) * CHUNK)
                q_ref[kv, 0:128, cols] = turned[:, tokens]
                q_ref[kv, 128:256, cols] = penalty[:, tokens]
        k_ref[kv] = rotated(keys, kv).astype(bf16)
        v_ref[kv] = jnp.transpose(values[:, kv * 128 : (kv + 1) * 128].astype(f32)).astype(bf16)


def prepare(lengths, first, queries, keys, values):
    inverse = inverse_frequencies()
    inverse = jnp.concatenate([inverse, inverse])[None, :]
    smem = pl.BlockSpec(memory_space=pltpu.SMEM)
    vmem = pl.BlockSpec(memory_space=pltpu.VMEM)
    return pl.pallas_call(
        prepare_kernel,
        out_shape=(
            jax.ShapeDtypeStruct((2, 256, GROUP * HALF), bf16),
            jax.ShapeDtypeStruct((2, HALF, 128), bf16),
            jax.ShapeDtypeStruct((2, 128, HALF), bf16),
        ),
        in_specs=[smem, smem, vmem, vmem, vmem, vmem],
        out_specs=(vmem, vmem, vmem),
        compiler_params=pltpu.CompilerParams(vmem_limit_bytes=40 * 2**20),
    )(lengths, first, inverse, queries, keys, values)


def main_kernel(
    bounds, qp, kp, vp, w_hbm, o_ref,
    q, kbuf, vbuf, top, total, acc, wbuf, att, given, taken, s_even, s_odd,
    local_sem, swap_send, swap_recv, k_send, k_recv, v_send, v_recv,
    w_send, w_recv, z_send, z_recv, c_send, c_recv, a_send, a_recv, p_send, p_recv,
):
    ctx = lax.axis_index("ctx")
    z = lax.axis_index("head")
    core = lax.rem(ctx, 2)
    chip = ctx // 2
    x = lax.rem(chip, 4)
    y = chip // 4
    other = 1 - core
    mate = (ctx + 1 - 2 * core, z)

    def at(x_, y_):
        return ((y_ * 4 + x_) * 2 + core, z)

    def remote(src, dst, send, recv, device):
        return pltpu.make_async_remote_copy(
            src_ref=src, dst_ref=dst, send_sem=send, recv_sem=recv, device_id=device, device_id_type=MESH
        )

    begin, end = bounds[0:1, :], bounds[1:2, :]

    def mark(slot):
        where = (chip - slot) * BLOCK + lax.broadcasted_iota(jnp.int32, (BLOCK, 128), 0)
        kbuf[slot, :, 128:256] = jnp.where((where >= begin) & (where < end), 1.0, 0.0).astype(bf16)

    barrier = pltpu.get_barrier_semaphore()
    pl.semaphore_signal(barrier, inc=1, device_id=mate, device_id_type=MESH)
    for step in (1, 2, 3):
        for device in (
            at(lax.rem(x + step, 4), y),
            at(x, lax.rem(y + step, 4)),
            (ctx, lax.rem(z + step, 4)),
        ):
            pl.semaphore_signal(barrier, inc=1, device_id=device, device_id_type=MESH)
    pl.semaphore_wait(barrier, 10)

    mine = pl.ds(pl.multiple_of(core * HALF, HALF), HALF)
    mine_q = pl.ds(pl.multiple_of(core * GROUP * HALF, GROUP * HALF), GROUP * HALF)
    swaps = [
        remote(kp.at[other], kbuf.at[0, mine, pl.ds(0, 128)], swap_send.at[0], swap_recv.at[0], mate),
        remote(vp.at[other], vbuf.at[0, :, mine], swap_send.at[1], swap_recv.at[1], mate),
        remote(qp.at[other], q.at[:, mine_q], swap_send.at[2], swap_recv.at[2], mate),
    ]
    for copy in swaps:
        copy.start()
    first_row = core * HALF

    def from_hbm(t, row, count):
        return w_hbm.at[
            pl.ds(pl.multiple_of(first_row + row, 64), count),
            pl.ds(pl.multiple_of(lax.rem(z + t, 4) * 2048, 2048), 2048),
        ]

    w_own = pltpu.make_async_copy(from_hbm(0, 0, HALF), wbuf.at[0], local_sem.at[3])
    w_whole = [
        remote(from_hbm(t, 0, 256), wbuf.at[t, pl.ds(0, 256), :], w_send.at[i], w_recv.at[i], (ctx, lax.rem(z + t, 4)))
        for i, t in enumerate((1, 3))
    ]

    def piece_of(t, which):
        size, base = (128, 0) if t == 2 else (64, 256)
        return pl.ds(pl.multiple_of(base + which * size, 64), size)

    def own_piece(t):
        return y if t == 2 else x

    w_pieces, w_spread, w_awaited = [], [], []
    for i, t in enumerate((2, 1, 3)):
        size, base = (128, 0) if t == 2 else (64, 256)
        held = wbuf.at[t, piece_of(t, own_piece(t)), :]
        w_pieces.append(
            remote(
                from_hbm(t, base + own_piece(t) * size, size), held,
                z_send.at[i], z_recv.at[i], (ctx, lax.rem(z + t, 4)),
            )
        )
        for step in (1, 2, 3):
            to = lax.rem(own_piece(t) + step, 4)
            device = at(x, to) if t == 2 else at(to, y)
            w_spread.append(remote(held, held, c_send.at[i, step - 1], c_recv.at[i, step - 1], device))
            came = lax.rem(own_piece(t) + 4 - step, 4)
            w_awaited.append(
                remote(held, wbuf.at[t, piece_of(t, came), :], c_send.at[i, step - 1], c_recv.at[i, step - 1], mate)
            )

    def spread_weights():
        for copy in w_pieces:
            copy.wait_recv()
        for copy in w_spread:
            copy.start()

    locals_ = [
        pltpu.make_async_copy(kp.at[core], kbuf.at[0, mine, pl.ds(0, 128)], local_sem.at[0]),
        pltpu.make_async_copy(vp.at[core], vbuf.at[0, :, mine], local_sem.at[1]),
        pltpu.make_async_copy(qp.at[core], q.at[:, mine_q], local_sem.at[2]),
    ]
    for copy in locals_:
        copy.start()
    for copy in w_pieces + w_whole:
        copy.start()
    w_own.start()
    mark(0)

    def share(slot, far, device, index):
        return (
            remote(kbuf.at[slot, :, pl.ds(0, 128)], kbuf.at[far, :, pl.ds(0, 128)], k_send.at[index], k_recv.at[far], device),
            remote(vbuf.at[slot], vbuf.at[far], v_send.at[index], v_recv.at[far], device),
        )

    below = at(x, lax.rem(y + 1, 4))
    own = [(y <= 2, share(0, 4, below, 0))]
    second = [((y >= 1) & (y <= 2), share(4, 8, below, 1))]
    third = []
    for step in (1, 3, 2):
        x_ = lax.rem(x + step, 4)
        near = step != 2
        own.append((x_ > x, share(0, lax.rem(4 + x_ - x, 4), at(x_, y), 1 + step)))
        second.append((y >= 1 if near else (y >= 1) & (x_ < x), share(4, 4 + x_ - x, at(x_, y), 4 + step)))
        if near:
            third.append(((y >= 2) & (x_ < x), share(8, lax.rem(8 + x_ - x, 9), at(x_, y), 7 + step)))
    down = [((y <= 2) & (chip >= 2), share(2, 6, below, 9))]

    def pass_on(list_, slot=None, rows_before=0):
        for part in (0, 1):
            if slot is not None:
                @pl.when(y >= rows_before)
                def _():
                    share(slot, slot, mate, 0)[part].wait_recv()
            for condition, copies in list_:
                @pl.when(condition)
                def _():
                    copies[part].start()

    def arrived(slot):
        @pl.when((slot != 4) & (slot != 8))
        def _():
            for copy in share(slot, slot, mate, 0):
                copy.wait_recv()

        @pl.when(slot == 2)
        def _():
            pass_on(down)

    for copy in swaps[:2]:
        copy.wait_recv()
    for copy in locals_[:2]:
        copy.wait()
    pass_on(own)
    for slot in range(1, SLOTS):
        mark(slot)
    swaps[2].wait_recv()
    locals_[2].wait()

    for chunk in range(CHUNKS):
        cols = slice(chunk * TILE, (chunk + 1) * TILE)
        seen = (chunk + 1) * CHUNK
        s = jnp.dot(kbuf[0, 0:seen, :], q[:, cols], preferred_element_type=f32)
        key = lax.broadcasted_iota(jnp.int32, s.shape, 0)
        query = chunk * CHUNK + lax.rem(lax.broadcasted_iota(jnp.int32, s.shape, 1), CHUNK)
        s = jnp.where(key <= query, s, neg_large)
        new = jnp.max(s, axis=0, keepdims=True)
        p = jnp.exp2((s - new) * exp2_scale)
        top[chunk] = new
        total[chunk] = jnp.sum(p, axis=0, keepdims=True)
        acc[chunk] = jnp.dot(vbuf[0, :, 0:seen], p.astype(bf16), preferred_element_type=f32)

    def scores(slot, chunk):
        cols = pl.ds(pl.multiple_of(chunk * TILE, TILE), TILE)
        return jnp.dot(kbuf[slot], q[:, cols], preferred_element_type=f32)

    def add(scores_ref, slot, chunk):
        s = scores_ref[...]
        old = top[chunk]
        new = jnp.maximum(old, jnp.max(s, axis=0, keepdims=True))
        p = jnp.exp2((s - new) * exp2_scale)
        scale = jnp.exp2((old - new) * exp2_scale)
        total[chunk] = total[chunk] * scale + jnp.sum(p, axis=0, keepdims=True)
        top[chunk] = new
        acc[chunk] = acc[chunk] * scale + jnp.dot(vbuf[slot], p.astype(bf16), preferred_element_type=f32)

    def slot_of(i):
        of_second = jnp.where(i < 4, i, i + 1)
        of_third = jnp.where(i == x + 4, 8, i)
        later = jnp.where(i == x, 4, jnp.where(i <= x + 3, of_second, of_third))
        return jnp.where(i < x, i + 1, later)

    def chunk_of(i):
        return lax.rem(i + 2 * other, CHUNKS)

    def sends(i):
        return [
            remote(att.at[i, 0], att.at[i, t], a_send.at[i, t], a_recv.at[i, t], (ctx, lax.rem(z + t, 4)))
            for t in (1, 3)
        ]

    def relays(i):
        copies = []
        for t, half, index in ((1, 0, 0), (3, 1, 2)):
            part = pl.ds(half * (CHUNK // 2), CHUNK // 2)
            copies.append(
                remote(
                    att.at[i, t, part, :], att.at[i, 2, part, :],
                    a_send.at[i, index], a_recv.at[i, index], (ctx, lax.rem(z + t, 4)),
                )
            )
        return copies

    def relay(i):
        for copy in sends(i):
            copy.wait_recv()
        for copy in relays(i):
            copy.start()

    def finish(i):
        chunk = chunk_of(i)
        out = acc[chunk] / total[chunk]
        for member in range(GROUP):
            cols = slice(member * CHUNK, (member + 1) * CHUNK)
            att[i, 0, :, member * 128 : (member + 1) * 128] = jnp.transpose(out[:, cols]).astype(bf16)
        for copy in sends(i):
            copy.start()

    pass_on(second, 4, 1)
    blocks = jnp.minimum(8, chip)

    @pl.when(blocks >= LAST)
    def _():
        arrived(slot_of(0))
        s_even[...] = scores(slot_of(0), jnp.where(blocks > LAST, 0, chunk_of(0)))

        def block_step(i, _):
            slot, later = slot_of(i), slot_of(i + 1)

            @pl.when(i == 1 + x // 2)
            def _():
                pass_on(third, 8, 2)

            s_odd[...] = scores(slot, 1)
            add(s_even, slot, 0)
            s_even[...] = scores(slot, 2)
            add(s_odd, slot, 1)
            arrived(later)
            s_odd[...] = scores(slot, 3)
            add(s_even, slot, 2)
            s_even[...] = scores(later, jnp.where(i + 1 < blocks - LAST, 0, chunk_of(0)))
            add(s_odd, slot, 3)
            return 0

        lax.fori_loop(0, blocks - LAST, block_step, 0)
        spread_weights()

        def chunk_step(i, _):
            chunk = chunk_of(i)
            slots = [slot_of(blocks - LAST + j) for j in range(LAST)]

            @pl.when(i >= 2)
            def _():
                relay(i - 2)

            for j in range(LAST):
                ready, coming = (s_even, s_odd) if j % 2 == 0 else (s_odd, s_even)
                if j + 1 < LAST:
                    @pl.when(i == 0)
                    def _():
                        arrived(slots[j + 1])

                    coming[...] = scores(slots[j + 1], chunk)
                else:
                    coming[...] = scores(slots[0], chunk_of(i + 1))
                add(ready, slots[j], chunk)
            finish(i)
            return 0

        lax.fori_loop(0, CHUNKS, chunk_step, 0)

    @pl.when(blocks < LAST)
    def _():
        def block_here(j, _):
            arrived(slot_of(j))
            return 0

        lax.fori_loop(0, blocks, block_here, 0)
        spread_weights()

        def chunk_step(i, _):
            def one(j, _):
                s_even[...] = scores(slot_of(j), chunk_of(i))
                add(s_even, slot_of(j), chunk_of(i))
                return 0

            @pl.when(i >= 2)
            def _():
                relay(i - 2)

            lax.fori_loop(0, blocks, one, 0)
            finish(i)
            return 0

        lax.fori_loop(0, CHUNKS, chunk_step, 0)

    relay(2)
    w_own.wait()
    for copy in w_whole:
        copy.wait_recv()
    for copy in w_awaited:
        copy.wait_recv()

    def exchange(i):
        return remote(given.at[i], taken.at[i], p_send.at[i], p_recv.at[i], mate)

    def project(i, keep):
        for copy in relays(i):
            copy.wait_recv()

        def some(n, _):
            cols = pl.ds(pl.multiple_of(n * 512, 512), 512)
            part = jnp.dot(att[i, 0], wbuf[0, :, cols], preferred_element_type=f32)
            for s in (1, 2, 3):
                part = part + jnp.dot(att[i, s], wbuf[s, :, cols], preferred_element_type=f32)
            keep(cols, part)
            return 0

        lax.fori_loop(0, 4, some, 0)

    for i in (0, 1):
        def give(cols, part):
            given[i, :, cols] = part

        project(i, give)
        exchange(i).start()
        if i == 0:
            relay(3)
    for i in (0, 1):
        exchange(i).wait_recv()

        def keep(cols, part):
            o_ref[i * CHUNK : (i + 1) * CHUNK, cols] = (part + taken[i, :, cols]).astype(bf16)

        project(i + 2, keep)

    for copy in swaps + w_whole + w_pieces + w_spread:
        copy.wait_send()
    for list_ in (own, second, third, down):
        for condition, copies in list_:
            @pl.when(condition)
            def _():
                for copy in copies:
                    copy.wait_send()
    for i in range(CHUNKS):
        for copy in sends(i) + relays(i):
            copy.wait_send()
    for i in (0, 1):
        exchange(i).wait_send()


def attend_and_project(bounds, q, k, v, out_weight):
    vmem = pl.BlockSpec(memory_space=pltpu.VMEM)
    dma = pltpu.SemaphoreType.DMA
    return pl.pallas_call(
        main_kernel,
        out_shape=jax.ShapeDtypeStruct((HALF, 2048), bf16),
        in_specs=[vmem, vmem, vmem, vmem, pl.BlockSpec(memory_space=pl.ANY)],
        out_specs=vmem,
        scratch_shapes=[
            pltpu.VMEM((256, GROUP * BLOCK), bf16),
            pltpu.VMEM((SLOTS, BLOCK, 256), bf16),
            pltpu.VMEM((SLOTS, 128, BLOCK), bf16),
            pltpu.VMEM((CHUNKS, 1, TILE), f32),
            pltpu.VMEM((CHUNKS, 1, TILE), f32),
            pltpu.VMEM((CHUNKS, 128, TILE), f32),
            pltpu.VMEM((4, HALF, 2048), bf16),
            pltpu.VMEM((CHUNKS, 4, CHUNK, 512), bf16),
            pltpu.VMEM((2, CHUNK, 2048), f32),
            pltpu.VMEM((2, CHUNK, 2048), f32),
            pltpu.VMEM((BLOCK, TILE), f32),
            pltpu.VMEM((BLOCK, TILE), f32),
            dma((4,)), dma((3,)), dma((3,)),
            dma((11,)), dma((SLOTS,)), dma((11,)), dma((SLOTS,)),
            dma((2,)), dma((2,)), dma((3,)), dma((3,)), dma((3, 3)), dma((3, 3)),
            dma((CHUNKS, 4)), dma((CHUNKS, 4)), dma((2,)), dma((2,)),
        ],
        compiler_params=pltpu.CompilerParams(
            collective_id=0, has_side_effects=True, vmem_limit_bytes=60 * 2**20
        ),
    )(bounds, q, k, v, out_weight)


def per_device(queries, keys, values, lengths, out_weight):
    device = lax.axis_index("ctx")
    starts, ends = doc_bounds(lengths)
    bounds = jnp.pad(jnp.stack([starts, ends]), ((0, 6), (0, 128 - NDOCS)))
    first = (device * HALF).astype(jnp.int32).reshape(1)
    q, k, v = prepare(lengths, first, queries, keys, values)
    return attend_and_project(bounds, q, k, v, out_weight)


def solution(mesh):
    return jax.shard_map(
        per_device,
        mesh=mesh,
        in_specs=(P("ctx", "head"), P("ctx", "head"), P("ctx", "head"), P(), P("head", None)),
        out_specs=P("ctx", "head"),
        check_vma=False,
    )
```

```python
import math

import jax
import jax.numpy as jnp
from jax import lax
from jax.experimental import pallas as pl
from jax.experimental.pallas import tpu as pltpu
from jax.sharding import PartitionSpec as P

f32, bf16 = jnp.float32, jnp.bfloat16
rope_base = 1000000.0
ramp_low = 23.0
ramp_high = 40.0
yarn_factor = 4.0
mscale = 0.1 * math.log(4.0) + 1.0
neg_large = -1e30
exp2_scale = math.log2(math.e) / math.sqrt(128.0)
doc_penalty = 131072.0

NDOCS = 8
BLOCK = 1024
GROUP = 4
HALF = 512
CHUNK = 256
TILE = GROUP * CHUNK
CHUNKS = BLOCK // CHUNK
SLOTS = 9
LAST = 4
MESH = pl.DeviceIdType.MESH


def inverse_frequencies():
    pair_index = jnp.arange(64).astype(f32)
    extrap = jnp.exp(-(2.0 * pair_index / 128.0) * math.log(rope_base))
    ramp = jnp.clip((pair_index - ramp_low) / (ramp_high - ramp_low), 0.0, 1.0)
    return extrap / yarn_factor * ramp + extrap * (1.0 - ramp)


def prepare_kernel(lengths, first_ref, inverse, queries, keys, values, q_ref, k_ref, v_ref, bounds_ref):
    first = first_ref[0] + pl.program_id(0) * CHUNK
    lane = lax.broadcasted_iota(jnp.int32, (CHUNK, 128), 1)
    at = first + lax.broadcasted_iota(jnp.int32, (CHUNK, 128), 0)
    start = jnp.zeros((CHUNK, 128), jnp.int32)
    document = lax.broadcasted_iota(jnp.int32, (128, CHUNK), 0)
    across = first + lax.broadcasted_iota(jnp.int32, (128, CHUNK), 1)
    hidden = document < NDOCS
    bound_row = lax.broadcasted_iota(jnp.int32, (8, 128), 0)
    bound_lane = lax.broadcasted_iota(jnp.int32, (8, 128), 1)
    bounds = jnp.zeros((8, 128), jnp.int32)
    end = 0
    for j in range(NDOCS):
        begin, end = end, end + lengths[j]
        start = start + jnp.where(at >= end, lengths[j], 0)
        hidden = hidden & ~((document == j) & (across >= begin) & (across < end))
        bounds = jnp.where((bound_lane == j) & (bound_row == 0), begin, bounds)
        bounds = jnp.where((bound_lane == j) & (bound_row == 1), end, bounds)
    bounds_ref[...] = bounds
    penalty = jnp.where(hidden, -doc_penalty, 0.0).astype(bf16)
    angles = (at - start).astype(f32) * inverse[...]
    cosine = jnp.cos(angles) * mscale
    sine = jnp.sin(angles) * mscale
    sine = jnp.where(lane < 64, -sine, sine)

    def rotated(ref, head):
        x = ref[:, head * 128 : (head + 1) * 128].astype(f32)
        return x * cosine + pltpu.roll(x, 64, 1) * sine

    for kv in range(2):
        for member in range(GROUP):
            cols = slice(member * CHUNK, (member + 1) * CHUNK)
            q_ref[kv, 0:128, cols] = jnp.transpose(rotated(queries, kv * GROUP + member)).astype(bf16)
            q_ref[kv, 128:256, cols] = penalty
        k_ref[kv] = rotated(keys, kv).astype(bf16)
        v_ref[kv] = jnp.transpose(values[:, kv * 128 : (kv + 1) * 128].astype(f32)).astype(bf16)


def prepare(lengths, first, queries, keys, values):
    inverse = inverse_frequencies()
    inverse = jnp.concatenate([inverse, inverse])[None, :]
    smem = pl.BlockSpec(memory_space=pltpu.SMEM)
    return pl.pallas_call(
        prepare_kernel,
        grid=(HALF // CHUNK,),
        out_shape=(
            jax.ShapeDtypeStruct((2, 256, GROUP * HALF), bf16),
            jax.ShapeDtypeStruct((2, HALF, 128), bf16),
            jax.ShapeDtypeStruct((2, 128, HALF), bf16),
            jax.ShapeDtypeStruct((8, 128), jnp.int32),
        ),
        in_specs=[
            smem,
            smem,
            pl.BlockSpec((1, 128), lambda i: (0, 0)),
            pl.BlockSpec((CHUNK, 1024), lambda i: (i, 0)),
            pl.BlockSpec((CHUNK, 256), lambda i: (i, 0)),
            pl.BlockSpec((CHUNK, 256), lambda i: (i, 0)),
        ],
        out_specs=(
            pl.BlockSpec((2, 256, TILE), lambda i: (0, 0, i)),
            pl.BlockSpec((2, CHUNK, 128), lambda i: (0, i, 0)),
            pl.BlockSpec((2, 128, CHUNK), lambda i: (0, 0, i)),
            pl.BlockSpec((8, 128), lambda i: (0, 0)),
        ),
        compiler_params=pltpu.CompilerParams(vmem_limit_bytes=62 * 2**20),
    )(lengths, first, inverse, queries, keys, values)


def main_kernel(
    bounds, qp, kp, vp, w_hbm, o_ref,
    q, kbuf, vbuf, top, total, acc, wbuf, att, given, taken, s_even, s_odd,
    local_sem, swap_send, swap_recv, k_send, k_recv, v_send, v_recv,
    w_send, w_recv, z_send, z_recv, c_send, c_recv, a_send, a_recv, p_send, p_recv,
):
    ctx = lax.axis_index("ctx")
    z = lax.axis_index("head")
    core = lax.rem(ctx, 2)
    chip = ctx // 2
    x = lax.rem(chip, 4)
    y = chip // 4
    other = 1 - core
    mate = (ctx + 1 - 2 * core, z)

    def at(x_, y_):
        return ((y_ * 4 + x_) * 2 + core, z)

    def remote(src, dst, send, recv, device):
        return pltpu.make_async_remote_copy(
            src_ref=src, dst_ref=dst, send_sem=send, recv_sem=recv, device_id=device, device_id_type=MESH
        )

    begin, end = bounds[0:1, :], bounds[1:2, :]

    def mark(slot):
        where = (chip - slot) * BLOCK + lax.broadcasted_iota(jnp.int32, (BLOCK, 128), 0)
        kbuf[slot, :, 128:256] = jnp.where((where >= begin) & (where < end), 1.0, 0.0).astype(bf16)

    barrier = pltpu.get_barrier_semaphore()
    pl.semaphore_signal(barrier, inc=1, device_id=mate, device_id_type=MESH)
    for step in (1, 2, 3):
        for device in (
            at(lax.rem(x + step, 4), y),
            at(x, lax.rem(y + step, 4)),
            (ctx, lax.rem(z + step, 4)),
        ):
            pl.semaphore_signal(barrier, inc=1, device_id=device, device_id_type=MESH)
    pl.semaphore_wait(barrier, 10)

    mine = pl.ds(pl.multiple_of(core * HALF, HALF), HALF)
    mine_q = pl.ds(pl.multiple_of(core * GROUP * HALF, GROUP * HALF), GROUP * HALF)
    swaps = [
        remote(kp.at[other], kbuf.at[0, mine, pl.ds(0, 128)], swap_send.at[0], swap_recv.at[0], mate),
        remote(vp.at[other], vbuf.at[0, :, mine], swap_send.at[1], swap_recv.at[1], mate),
        remote(qp.at[other], q.at[:, mine_q], swap_send.at[2], swap_recv.at[2], mate),
    ]
    for copy in swaps:
        copy.start()
    first_row = core * HALF

    def from_hbm(t, row, count):
        return w_hbm.at[
            pl.ds(pl.multiple_of(first_row + row, 64), count),
            pl.ds(pl.multiple_of(lax.rem(z + t, 4) * 2048, 2048), 2048),
        ]

    w_own = pltpu.make_async_copy(from_hbm(0, 0, HALF), wbuf.at[0], local_sem.at[3])
    w_whole = [
        remote(from_hbm(t, 0, 256), wbuf.at[t, pl.ds(0, 256), :], w_send.at[i], w_recv.at[i], (ctx, lax.rem(z + t, 4)))
        for i, t in enumerate((1, 3))
    ]

    def piece_of(t, which):
        size, base = (128, 0) if t == 2 else (64, 256)
        return pl.ds(pl.multiple_of(base + which * size, 64), size)

    def own_piece(t):
        return y if t == 2 else x

    w_pieces, w_spread, w_awaited = [], [], []
    for i, t in enumerate((2, 1, 3)):
        size, base = (128, 0) if t == 2 else (64, 256)
        held = wbuf.at[t, piece_of(t, own_piece(t)), :]
        w_pieces.append(
            remote(
                from_hbm(t, base + own_piece(t) * size, size), held,
                z_send.at[i], z_recv.at[i], (ctx, lax.rem(z + t, 4)),
            )
        )
        for step in (1, 2, 3):
            to = lax.rem(own_piece(t) + step, 4)
            device = at(x, to) if t == 2 else at(to, y)
            w_spread.append(remote(held, held, c_send.at[i, step - 1], c_recv.at[i, step - 1], device))
            came = lax.rem(own_piece(t) + 4 - step, 4)
            w_awaited.append(
                remote(held, wbuf.at[t, piece_of(t, came), :], c_send.at[i, step - 1], c_recv.at[i, step - 1], mate)
            )

    def spread_weights():
        for copy in w_pieces:
            copy.wait_recv()
        for copy in w_spread:
            copy.start()

    locals_ = [
        pltpu.make_async_copy(kp.at[core], kbuf.at[0, mine, pl.ds(0, 128)], local_sem.at[0]),
        pltpu.make_async_copy(vp.at[core], vbuf.at[0, :, mine], local_sem.at[1]),
        pltpu.make_async_copy(qp.at[core], q.at[:, mine_q], local_sem.at[2]),
    ]
    for copy in locals_:
        copy.start()
    for copy in w_pieces + w_whole:
        copy.start()
    w_own.start()
    mark(0)

    def share(slot, far, device, index):
        return (
            remote(kbuf.at[slot, :, pl.ds(0, 128)], kbuf.at[far, :, pl.ds(0, 128)], k_send.at[index], k_recv.at[far], device),
            remote(vbuf.at[slot], vbuf.at[far], v_send.at[index], v_recv.at[far], device),
        )

    below = at(x, lax.rem(y + 1, 4))
    own = [(y <= 2, share(0, 4, below, 0))]
    second = [((y >= 1) & (y <= 2), share(4, 8, below, 1))]
    third = []
    for step in (1, 3, 2):
        x_ = lax.rem(x + step, 4)
        near = step != 2
        own.append((x_ > x, share(0, lax.rem(4 + x_ - x, 4), at(x_, y), 1 + step)))
        second.append((y >= 1 if near else (y >= 1) & (x_ < x), share(4, 4 + x_ - x, at(x_, y), 4 + step)))
        if near:
            third.append(((y >= 2) & (x_ < x), share(8, lax.rem(8 + x_ - x, 9), at(x_, y), 7 + step)))
    down = [((y <= 2) & (chip >= 2), share(2, 6, below, 9))]

    def pass_on(list_, slot=None, rows_before=0):
        for part in (0, 1):
            if slot is not None:
                @pl.when(y >= rows_before)
                def _():
                    share(slot, slot, mate, 0)[part].wait_recv()
            for condition, copies in list_:
                @pl.when(condition)
                def _():
                    copies[part].start()

    def arrived(slot):
        @pl.when((slot != 4) & (slot != 8))
        def _():
            for copy in share(slot, slot, mate, 0):
                copy.wait_recv()

        @pl.when(slot == 2)
        def _():
            pass_on(down)

        @pl.when(slot == 8)
        def _():
            pass_on(third, 8, 2)

    for copy in swaps[:2]:
        copy.wait_recv()
    for copy in locals_[:2]:
        copy.wait()
    pass_on(own)
    for slot in range(1, SLOTS):
        mark(slot)
    swaps[2].wait_recv()
    locals_[2].wait()

    for chunk in range(CHUNKS):
        cols = slice(chunk * TILE, (chunk + 1) * TILE)
        seen = (chunk + 1) * CHUNK
        s = jnp.dot(kbuf[0, 0:seen, :], q[:, cols], preferred_element_type=f32)
        key = lax.broadcasted_iota(jnp.int32, s.shape, 0)
        query = chunk * CHUNK + lax.rem(lax.broadcasted_iota(jnp.int32, s.shape, 1), CHUNK)
        s = jnp.where(key <= query, s, neg_large)
        new = jnp.max(s, axis=0, keepdims=True)
        p = jnp.exp2((s - new) * exp2_scale)
        top[chunk] = new
        total[chunk] = jnp.sum(p, axis=0, keepdims=True)
        acc[chunk] = jnp.dot(vbuf[0, :, 0:seen], p.astype(bf16), preferred_element_type=f32)

    def scores(slot, chunk):
        cols = pl.ds(pl.multiple_of(chunk * TILE, TILE), TILE)
        return jnp.dot(kbuf[slot], q[:, cols], preferred_element_type=f32)

    def add(scores_ref, slot, chunk):
        s = scores_ref[...]
        old = top[chunk]
        new = jnp.maximum(old, jnp.max(s, axis=0, keepdims=True))
        p = jnp.exp2((s - new) * exp2_scale)
        scale = jnp.exp2((old - new) * exp2_scale)
        total[chunk] = total[chunk] * scale + jnp.sum(p, axis=0, keepdims=True)
        top[chunk] = new
        acc[chunk] = acc[chunk] * scale + jnp.dot(vbuf[slot], p.astype(bf16), preferred_element_type=f32)

    def slot_of(i):
        shift = jnp.where(y >= 2, 1, 0)
        j = i - shift
        of_second = jnp.where(j < 4, j, j + 1)
        rest = jnp.where(j <= x + 3, of_second, i)
        column = jnp.where(i == x, 4, jnp.where((y >= 2) & (i == x + 1), 8, rest))
        return jnp.where(i < x, i + 1, column)

    def chunk_of(i):
        return lax.rem(i + 2 * other, CHUNKS)

    def sends(i):
        return [
            remote(att.at[i, 0], att.at[i, t], a_send.at[i, t], a_recv.at[i, t], (ctx, lax.rem(z + t, 4)))
            for t in (1, 3)
        ]

    def relays(i):
        copies = []
        for t, half, index in ((1, 0, 0), (3, 1, 2)):
            part = pl.ds(half * (CHUNK // 2), CHUNK // 2)
            copies.append(
                remote(
                    att.at[i, t, part, :], att.at[i, 2, part, :],
                    a_send.at[i, index], a_recv.at[i, index], (ctx, lax.rem(z + t, 4)),
                )
            )
        return copies

    def relay(i):
        for copy in sends(i):
            copy.wait_recv()
        for copy in relays(i):
            copy.start()

    def finish(i):
        chunk = chunk_of(i)
        out = acc[chunk] / total[chunk]
        for member in range(GROUP):
            cols = slice(member * CHUNK, (member + 1) * CHUNK)
            att[i, 0, :, member * 128 : (member + 1) * 128] = jnp.transpose(out[:, cols]).astype(bf16)
        for copy in sends(i):
            copy.start()

    pass_on(second, 4, 1)
    blocks = jnp.minimum(8, chip)

    @pl.when(blocks >= LAST)
    def _():
        arrived(slot_of(0))
        s_even[...] = scores(slot_of(0), jnp.where(blocks > LAST, 0, chunk_of(0)))

        def block_step(i, _):
            slot, later = slot_of(i), slot_of(i + 1)

            s_odd[...] = scores(slot, 1)
            add(s_even, slot, 0)
            s_even[...] = scores(slot, 2)
            add(s_odd, slot, 1)
            arrived(later)
            s_odd[...] = scores(slot, 3)
            add(s_even, slot, 2)
            s_even[...] = scores(later, jnp.where(i + 1 < blocks - LAST, 0, chunk_of(0)))
            add(s_odd, slot, 3)
            return 0

        lax.fori_loop(0, blocks - LAST, block_step, 0)

        def chunk_step(i, _):
            chunk = chunk_of(i)
            slots = [slot_of(blocks - LAST + j) for j in range(LAST)]

            @pl.when(i == 1)
            def _():
                spread_weights()

            @pl.when(i >= 2)
            def _():
                relay(i - 2)

            for j in range(LAST):
                ready, coming = (s_even, s_odd) if j % 2 == 0 else (s_odd, s_even)
                if j + 1 < LAST:
                    @pl.when(i == 0)
                    def _():
                        arrived(slots[j + 1])

                    coming[...] = scores(slots[j + 1], chunk)
                else:
                    coming[...] = scores(slots[0], chunk_of(i + 1))
                add(ready, slots[j], chunk)
            finish(i)
            return 0

        lax.fori_loop(0, CHUNKS, chunk_step, 0)

    @pl.when(blocks < LAST)
    def _():
        def block_here(j, _):
            arrived(slot_of(j))
            return 0

        lax.fori_loop(0, blocks, block_here, 0)

        def chunk_step(i, _):
            def one(j, _):
                s_even[...] = scores(slot_of(j), chunk_of(i))
                add(s_even, slot_of(j), chunk_of(i))
                return 0

            @pl.when(i == 1)
            def _():
                spread_weights()

            @pl.when(i >= 2)
            def _():
                relay(i - 2)

            lax.fori_loop(0, blocks, one, 0)
            finish(i)
            return 0

        lax.fori_loop(0, CHUNKS, chunk_step, 0)

    relay(2)
    w_own.wait()
    for copy in w_whole:
        copy.wait_recv()
    for copy in w_awaited:
        copy.wait_recv()

    def exchange(i):
        return remote(given.at[i], taken.at[i], p_send.at[i], p_recv.at[i], mate)

    def project(i, keep):
        for copy in relays(i):
            copy.wait_recv()

        def some(n, _):
            cols = pl.ds(pl.multiple_of(n * 512, 512), 512)
            part = jnp.dot(att[i, 0], wbuf[0, :, cols], preferred_element_type=f32)
            for s in (1, 2, 3):
                part = part + jnp.dot(att[i, s], wbuf[s, :, cols], preferred_element_type=f32)
            keep(cols, part)
            return 0

        lax.fori_loop(0, 4, some, 0)

    for i in (0, 1):
        def give(cols, part):
            given[i, :, cols] = part

        project(i, give)
        exchange(i).start()
        if i == 0:
            relay(3)
    for i in (0, 1):
        exchange(i).wait_recv()

        def keep(cols, part):
            o_ref[i * CHUNK : (i + 1) * CHUNK, cols] = (part + taken[i, :, cols]).astype(bf16)

        project(i + 2, keep)

    for copy in swaps + w_whole + w_pieces + w_spread:
        copy.wait_send()
    for list_ in (own, second, third, down):
        for condition, copies in list_:
            @pl.when(condition)
            def _():
                for copy in copies:
                    copy.wait_send()
    for i in range(CHUNKS):
        for copy in sends(i) + relays(i):
            copy.wait_send()
    for i in (0, 1):
        exchange(i).wait_send()


def attend_and_project(bounds, q, k, v, out_weight):
    vmem = pl.BlockSpec(memory_space=pltpu.VMEM)
    dma = pltpu.SemaphoreType.DMA
    return pl.pallas_call(
        main_kernel,
        out_shape=jax.ShapeDtypeStruct((HALF, 2048), bf16),
        in_specs=[vmem] + [pl.BlockSpec(memory_space=pl.ANY)] * 4,
        out_specs=vmem,
        scratch_shapes=[
            pltpu.VMEM((256, GROUP * BLOCK), bf16),
            pltpu.VMEM((SLOTS, BLOCK, 256), bf16),
            pltpu.VMEM((SLOTS, 128, BLOCK), bf16),
            pltpu.VMEM((CHUNKS, 1, TILE), f32),
            pltpu.VMEM((CHUNKS, 1, TILE), f32),
            pltpu.VMEM((CHUNKS, 128, TILE), f32),
            pltpu.VMEM((4, HALF, 2048), bf16),
            pltpu.VMEM((CHUNKS, 4, CHUNK, 512), bf16),
            pltpu.VMEM((2, CHUNK, 2048), f32),
            pltpu.VMEM((2, CHUNK, 2048), f32),
            pltpu.VMEM((BLOCK, TILE), f32),
            pltpu.VMEM((BLOCK, TILE), f32),
            dma((4,)), dma((3,)), dma((3,)),
            dma((11,)), dma((SLOTS,)), dma((11,)), dma((SLOTS,)),
            dma((2,)), dma((2,)), dma((3,)), dma((3,)), dma((3, 3)), dma((3, 3)),
            dma((CHUNKS, 4)), dma((CHUNKS, 4)), dma((2,)), dma((2,)),
        ],
        compiler_params=pltpu.CompilerParams(
            collective_id=0, has_side_effects=True, vmem_limit_bytes=60 * 2**20
        ),
    )(bounds, q, k, v, out_weight)


def per_device(queries, keys, values, lengths, out_weight):
    device = lax.axis_index("ctx")
    first = (device * HALF).astype(jnp.int32).reshape(1)
    q, k, v, bounds = prepare(lengths, first, queries, keys, values)
    return attend_and_project(bounds, q, k, v, out_weight)


def solution(mesh):
    return jax.shard_map(
        per_device,
        mesh=mesh,
        in_specs=(P("ctx", "head"), P("ctx", "head"), P("ctx", "head"), P(), P("head", None)),
        out_specs=P("ctx", "head"),
        check_vma=False,
    )
```

```python
import math

import jax
import jax.numpy as jnp
from jax import lax
from jax.experimental import pallas as pl
from jax.experimental.pallas import tpu as pltpu
from jax.sharding import PartitionSpec as P

f32, bf16 = jnp.float32, jnp.bfloat16
rope_base = 1000000.0
ramp_low = 23.0
ramp_high = 40.0
yarn_factor = 4.0
mscale = 0.1 * math.log(4.0) + 1.0
neg_large = -1e30
exp2_scale = math.log2(math.e) / math.sqrt(128.0)
doc_penalty = 131072.0

NDOCS = 8
BLOCK = 1024
GROUP = 4
HALF = 512
CHUNK = 256
TILE = GROUP * CHUNK
CHUNKS = BLOCK // CHUNK
SLOTS = 9
LAST = 4
MESH = pl.DeviceIdType.MESH


def inverse_frequencies():
    pair_index = jnp.arange(64).astype(f32)
    extrap = jnp.exp(-(2.0 * pair_index / 128.0) * math.log(rope_base))
    ramp = jnp.clip((pair_index - ramp_low) / (ramp_high - ramp_low), 0.0, 1.0)
    return extrap / yarn_factor * ramp + extrap * (1.0 - ramp)


def prepare_kernel(lengths, first_ref, inverse, queries, keys, values, q_ref, k_ref, v_ref, bounds_ref):
    first = first_ref[0] + pl.program_id(0) * CHUNK
    lane = lax.broadcasted_iota(jnp.int32, (CHUNK, 128), 1)
    at = first + lax.broadcasted_iota(jnp.int32, (CHUNK, 128), 0)
    start = jnp.zeros((CHUNK, 128), jnp.int32)
    document = lax.broadcasted_iota(jnp.int32, (128, CHUNK), 0)
    across = first + lax.broadcasted_iota(jnp.int32, (128, CHUNK), 1)
    hidden = document < NDOCS
    bound_row = lax.broadcasted_iota(jnp.int32, (8, 128), 0)
    bound_lane = lax.broadcasted_iota(jnp.int32, (8, 128), 1)
    bounds = jnp.zeros((8, 128), jnp.int32)
    end = 0
    for j in range(NDOCS):
        begin, end = end, end + lengths[j]
        start = start + jnp.where(at >= end, lengths[j], 0)
        hidden = hidden & ~((document == j) & (across >= begin) & (across < end))
        bounds = jnp.where((bound_lane == j) & (bound_row == 0), begin, bounds)
        bounds = jnp.where((bound_lane == j) & (bound_row == 1), end, bounds)
    bounds_ref[...] = bounds
    penalty = jnp.where(hidden, -doc_penalty, 0.0).astype(bf16)
    angles = (at - start).astype(f32) * inverse[...]
    cosine = jnp.cos(angles) * mscale
    sine = jnp.sin(angles) * mscale
    sine = jnp.where(lane < 64, -sine, sine)

    def rotated(ref, head):
        x = ref[:, head * 128 : (head + 1) * 128].astype(f32)
        return x * cosine + pltpu.roll(x, 64, 1) * sine

    for kv in range(2):
        for member in range(GROUP):
            cols = slice(member * CHUNK, (member + 1) * CHUNK)
            q_ref[kv, 0:128, cols] = jnp.transpose(rotated(queries, kv * GROUP + member)).astype(bf16)
            q_ref[kv, 128:256, cols] = penalty
        k_ref[kv] = rotated(keys, kv).astype(bf16)
        v_ref[kv] = jnp.transpose(values[:, kv * 128 : (kv + 1) * 128].astype(f32)).astype(bf16)


def prepare(lengths, first, queries, keys, values):
    inverse = inverse_frequencies()
    inverse = jnp.concatenate([inverse, inverse])[None, :]
    smem = pl.BlockSpec(memory_space=pltpu.SMEM)
    return pl.pallas_call(
        prepare_kernel,
        grid=(HALF // CHUNK,),
        out_shape=(
            jax.ShapeDtypeStruct((2, 256, GROUP * HALF), bf16),
            jax.ShapeDtypeStruct((2, HALF, 128), bf16),
            jax.ShapeDtypeStruct((2, 128, HALF), bf16),
            jax.ShapeDtypeStruct((8, 128), jnp.int32),
        ),
        in_specs=[
            smem,
            smem,
            pl.BlockSpec((1, 128), lambda i: (0, 0)),
            pl.BlockSpec((CHUNK, 1024), lambda i: (i, 0)),
            pl.BlockSpec((CHUNK, 256), lambda i: (i, 0)),
            pl.BlockSpec((CHUNK, 256), lambda i: (i, 0)),
        ],
        out_specs=(
            pl.BlockSpec((2, 256, TILE), lambda i: (0, 0, i)),
            pl.BlockSpec((2, CHUNK, 128), lambda i: (0, i, 0)),
            pl.BlockSpec((2, 128, CHUNK), lambda i: (0, 0, i)),
            pl.BlockSpec((8, 128), lambda i: (0, 0)),
        ),
        compiler_params=pltpu.CompilerParams(vmem_limit_bytes=62 * 2**20),
    )(lengths, first, inverse, queries, keys, values)


def main_kernel(
    bounds, qp, kp, vp, w_hbm, o_ref,
    q, kbuf, vbuf, top, total, acc, wbuf, att, given, taken, s_even, s_odd,
    local_sem, swap_send, swap_recv, k_send, k_recv, v_send, v_recv,
    w_send, w_recv, z_send, z_recv, c_send, c_recv, a_send, a_recv, p_send, p_recv,
):
    ctx = lax.axis_index("ctx")
    z = lax.axis_index("head")
    core = lax.rem(ctx, 2)
    chip = ctx // 2
    x = lax.rem(chip, 4)
    y = chip // 4
    other = 1 - core
    mate = (ctx + 1 - 2 * core, z)

    def at(x_, y_):
        return ((y_ * 4 + x_) * 2 + core, z)

    def remote(src, dst, send, recv, device):
        return pltpu.make_async_remote_copy(
            src_ref=src, dst_ref=dst, send_sem=send, recv_sem=recv, device_id=device, device_id_type=MESH
        )

    begin, end = bounds[0:1, :], bounds[1:2, :]

    def mark(slot):
        where = (chip - slot) * BLOCK + lax.broadcasted_iota(jnp.int32, (BLOCK, 128), 0)
        kbuf[slot, :, 128:256] = jnp.where((where >= begin) & (where < end), 1.0, 0.0).astype(bf16)

    barrier = pltpu.get_barrier_semaphore()
    pl.semaphore_signal(barrier, inc=1, device_id=mate, device_id_type=MESH)
    for step in (1, 2, 3):
        for device in (
            at(lax.rem(x + step, 4), y),
            at(x, lax.rem(y + step, 4)),
            (ctx, lax.rem(z + step, 4)),
        ):
            pl.semaphore_signal(barrier, inc=1, device_id=device, device_id_type=MESH)
    pl.semaphore_wait(barrier, 10)

    mine = pl.ds(pl.multiple_of(core * HALF, HALF), HALF)
    mine_q = pl.ds(pl.multiple_of(core * GROUP * HALF, GROUP * HALF), GROUP * HALF)
    swaps = [
        remote(kp.at[other], kbuf.at[0, mine, pl.ds(0, 128)], swap_send.at[0], swap_recv.at[0], mate),
        remote(vp.at[other], vbuf.at[0, :, mine], swap_send.at[1], swap_recv.at[1], mate),
        remote(qp.at[other], q.at[:, mine_q], swap_send.at[2], swap_recv.at[2], mate),
    ]
    for copy in swaps:
        copy.start()
    first_row = core * HALF

    def from_hbm(t, row, count):
        return w_hbm.at[
            pl.ds(pl.multiple_of(first_row + row, 64), count),
            pl.ds(pl.multiple_of(lax.rem(z + t, 4) * 2048, 2048), 2048),
        ]

    w_own = pltpu.make_async_copy(from_hbm(0, 0, HALF), wbuf.at[0], local_sem.at[3])
    w_whole = [
        remote(from_hbm(t, 0, 256), wbuf.at[t, pl.ds(0, 256), :], w_send.at[i], w_recv.at[i], (ctx, lax.rem(z + t, 4)))
        for i, t in enumerate((1, 3))
    ]

    def piece_of(t, which):
        size, base = (128, 0) if t == 2 else (64, 256)
        return pl.ds(pl.multiple_of(base + which * size, 64), size)

    def own_piece(t):
        return y if t == 2 else x

    w_pieces, w_spread, w_awaited = [], [], []
    for i, t in enumerate((2, 1, 3)):
        size, base = (128, 0) if t == 2 else (64, 256)
        held = wbuf.at[t, piece_of(t, own_piece(t)), :]
        w_pieces.append(
            remote(
                from_hbm(t, base + own_piece(t) * size, size), held,
                z_send.at[i], z_recv.at[i], (ctx, lax.rem(z + t, 4)),
            )
        )
        for step in (1, 2, 3) if t != 2 else ():
            to = lax.rem(own_piece(t) + step, 4)
            device = at(to, y)
            w_spread.append(remote(held, held, c_send.at[i, step - 1], c_recv.at[i, step - 1], device))
            came = lax.rem(own_piece(t) + 4 - step, 4)
            w_awaited.append(
                remote(held, wbuf.at[t, piece_of(t, came), :], c_send.at[i, step - 1], c_recv.at[i, step - 1], mate)
            )

    def spread_weights():
        for copy in w_pieces[1:]:
            copy.wait_recv()
        for copy in w_spread:
            copy.start()

    def down_y(k):
        held = wbuf.at[2, piece_of(2, lax.rem(y + k, 4)), :]
        return remote(held, held, c_send.at[0, k], c_recv.at[0, k], at(x, lax.rem(y + 3, 4)))

    def from_up_y(k):
        held = wbuf.at[2, piece_of(2, lax.rem(y + k + 1, 4)), :]
        return remote(held, held, c_send.at[0, k], c_recv.at[0, k], mate)

    def hand_on(k):
        (from_up_y(k - 1) if k else w_pieces[0]).wait_recv()
        down_y(k).start()

    locals_ = [
        pltpu.make_async_copy(kp.at[core], kbuf.at[0, mine, pl.ds(0, 128)], local_sem.at[0]),
        pltpu.make_async_copy(vp.at[core], vbuf.at[0, :, mine], local_sem.at[1]),
        pltpu.make_async_copy(qp.at[core], q.at[:, mine_q], local_sem.at[2]),
    ]
    for copy in locals_:
        copy.start()
    for copy in w_pieces + w_whole:
        copy.start()
    w_own.start()
    mark(0)

    def share(slot, far, device, index):
        return (
            remote(kbuf.at[slot, :, pl.ds(0, 128)], kbuf.at[far, :, pl.ds(0, 128)], k_send.at[index], k_recv.at[far], device),
            remote(vbuf.at[slot], vbuf.at[far], v_send.at[index], v_recv.at[far], device),
        )

    below = at(x, lax.rem(y + 1, 4))
    own = [(y <= 2, share(0, 4, below, 0))]
    second = [((y >= 1) & (y <= 2), share(4, 8, below, 1))]
    third = []
    for step in (1, 3, 2):
        x_ = lax.rem(x + step, 4)
        near = step != 2
        own.append((x_ > x, share(0, lax.rem(4 + x_ - x, 4), at(x_, y), 1 + step)))
        second.append((y >= 1 if near else (y >= 1) & (x_ < x), share(4, 4 + x_ - x, at(x_, y), 4 + step)))
        if near:
            third.append(((y >= 2) & (x_ < x), share(8, lax.rem(8 + x_ - x, 9), at(x_, y), 7 + step)))
    down = [((y <= 2) & (chip >= 2), share(2, 6, below, 9))]

    def pass_on(list_, slot=None, rows_before=0):
        for part in (0, 1):
            if slot is not None:
                @pl.when(y >= rows_before)
                def _():
                    share(slot, slot, mate, 0)[part].wait_recv()
            for condition, copies in list_:
                @pl.when(condition)
                def _():
                    copies[part].start()

    def arrived(slot):
        @pl.when((slot != 4) & (slot != 8))
        def _():
            for copy in share(slot, slot, mate, 0):
                copy.wait_recv()

        @pl.when(slot == 2)
        def _():
            pass_on(down)

        @pl.when(slot == 8)
        def _():
            pass_on(third, 8, 2)

    for copy in swaps[:2]:
        copy.wait_recv()
    for copy in locals_[:2]:
        copy.wait()
    pass_on(own)
    for slot in range(1, SLOTS):
        mark(slot)
    swaps[2].wait_recv()
    locals_[2].wait()

    for chunk in range(CHUNKS):
        cols = slice(chunk * TILE, (chunk + 1) * TILE)
        seen = (chunk + 1) * CHUNK
        s = jnp.dot(kbuf[0, 0:seen, :], q[:, cols], preferred_element_type=f32)
        key = lax.broadcasted_iota(jnp.int32, s.shape, 0)
        query = chunk * CHUNK + lax.rem(lax.broadcasted_iota(jnp.int32, s.shape, 1), CHUNK)
        s = jnp.where(key <= query, s, neg_large)
        new = jnp.max(s, axis=0, keepdims=True)
        p = jnp.exp2((s - new) * exp2_scale)
        top[chunk] = new
        total[chunk] = jnp.sum(p, axis=0, keepdims=True)
        acc[chunk] = jnp.dot(vbuf[0, :, 0:seen], p.astype(bf16), preferred_element_type=f32)

    def scores(slot, chunk):
        cols = pl.ds(pl.multiple_of(chunk * TILE, TILE), TILE)
        return jnp.dot(kbuf[slot], q[:, cols], preferred_element_type=f32)

    def add(scores_ref, slot, chunk):
        s = scores_ref[...]
        old = top[chunk]
        new = jnp.maximum(old, jnp.max(s, axis=0, keepdims=True))
        p = jnp.exp2((s - new) * exp2_scale)
        scale = jnp.exp2((old - new) * exp2_scale)
        total[chunk] = total[chunk] * scale + jnp.sum(p, axis=0, keepdims=True)
        top[chunk] = new
        acc[chunk] = acc[chunk] * scale + jnp.dot(vbuf[slot], p.astype(bf16), preferred_element_type=f32)

    def slot_of(i):
        shift = jnp.where(y >= 2, 1, 0)
        j = i - shift
        of_second = jnp.where(j < 4, j, j + 1)
        rest = jnp.where(j <= x + 3, of_second, i)
        column = jnp.where(i == x, 4, jnp.where((y >= 2) & (i == x + 1), 8, rest))
        return jnp.where(i < x, i + 1, column)

    def chunk_of(i):
        return lax.rem(i + 2 * other, CHUNKS)

    def sends(i):
        return [
            remote(att.at[i, 0], att.at[i, t], a_send.at[i, t], a_recv.at[i, t], (ctx, lax.rem(z + t, 4)))
            for t in (1, 3)
        ]

    def relays(i):
        copies = []
        for t, half, index in ((1, 0, 0), (3, 1, 2)):
            part = pl.ds(half * (CHUNK // 2), CHUNK // 2)
            copies.append(
                remote(
                    att.at[i, t, part, :], att.at[i, 2, part, :],
                    a_send.at[i, index], a_recv.at[i, index], (ctx, lax.rem(z + t, 4)),
                )
            )
        return copies

    def relay(i):
        for copy in sends(i):
            copy.wait_recv()
        for copy in relays(i):
            copy.start()

    def finish(i):
        chunk = chunk_of(i)
        out = acc[chunk] / total[chunk]
        for member in range(GROUP):
            cols = slice(member * CHUNK, (member + 1) * CHUNK)
            att[i, 0, :, member * 128 : (member + 1) * 128] = jnp.transpose(out[:, cols]).astype(bf16)
        for copy in sends(i):
            copy.start()

    pass_on(second, 4, 1)
    hand_on(0)
    blocks = jnp.minimum(8, chip)

    @pl.when(blocks >= LAST)
    def _():
        arrived(slot_of(0))
        s_even[...] = scores(slot_of(0), jnp.where(blocks > LAST, 0, chunk_of(0)))

        def block_step(i, _):
            slot, later = slot_of(i), slot_of(i + 1)

            s_odd[...] = scores(slot, 1)
            add(s_even, slot, 0)
            s_even[...] = scores(slot, 2)
            add(s_odd, slot, 1)
            arrived(later)
            s_odd[...] = scores(slot, 3)
            add(s_even, slot, 2)
            s_even[...] = scores(later, jnp.where(i + 1 < blocks - LAST, 0, chunk_of(0)))
            add(s_odd, slot, 3)
            return 0

        lax.fori_loop(0, blocks - LAST, block_step, 0)

        def chunk_step(i, _):
            chunk = chunk_of(i)
            slots = [slot_of(blocks - LAST + j) for j in range(LAST)]

            @pl.when(i == 0)
            def _():
                hand_on(1)

            @pl.when(i == 1)
            def _():
                spread_weights()
                hand_on(2)

            @pl.when(i >= 2)
            def _():
                relay(i - 2)

            for j in range(LAST):
                ready, coming = (s_even, s_odd) if j % 2 == 0 else (s_odd, s_even)
                if j + 1 < LAST:
                    @pl.when(i == 0)
                    def _():
                        arrived(slots[j + 1])

                    coming[...] = scores(slots[j + 1], chunk)
                else:
                    coming[...] = scores(slots[0], chunk_of(i + 1))
                add(ready, slots[j], chunk)
            finish(i)
            return 0

        lax.fori_loop(0, CHUNKS, chunk_step, 0)

    @pl.when(blocks < LAST)
    def _():
        def block_here(j, _):
            arrived(slot_of(j))
            return 0

        lax.fori_loop(0, blocks, block_here, 0)

        def chunk_step(i, _):
            def one(j, _):
                s_even[...] = scores(slot_of(j), chunk_of(i))
                add(s_even, slot_of(j), chunk_of(i))
                return 0

            @pl.when(i == 0)
            def _():
                hand_on(1)

            @pl.when(i == 1)
            def _():
                spread_weights()
                hand_on(2)

            @pl.when(i >= 2)
            def _():
                relay(i - 2)

            lax.fori_loop(0, blocks, one, 0)
            finish(i)
            return 0

        lax.fori_loop(0, CHUNKS, chunk_step, 0)

    relay(2)
    w_own.wait()
    for copy in w_whole:
        copy.wait_recv()
    for copy in w_awaited + [from_up_y(2)]:
        copy.wait_recv()

    def exchange(i):
        return remote(given.at[i], taken.at[i], p_send.at[i], p_recv.at[i], mate)

    def project(i, keep):
        for copy in relays(i):
            copy.wait_recv()

        def some(n, _):
            cols = pl.ds(pl.multiple_of(n * 512, 512), 512)
            part = jnp.dot(att[i, 0], wbuf[0, :, cols], preferred_element_type=f32)
            for s in (1, 2, 3):
                part = part + jnp.dot(att[i, s], wbuf[s, :, cols], preferred_element_type=f32)
            keep(cols, part)
            return 0

        lax.fori_loop(0, 4, some, 0)

    for i in (0, 1):
        def give(cols, part):
            given[i, :, cols] = part

        project(i, give)
        exchange(i).start()
        if i == 0:
            relay(3)
    for i in (0, 1):
        exchange(i).wait_recv()

        def keep(cols, part):
            o_ref[i * CHUNK : (i + 1) * CHUNK, cols] = (part + taken[i, :, cols]).astype(bf16)

        project(i + 2, keep)

    for copy in swaps + w_whole + w_pieces + w_spread + [down_y(k) for k in range(3)]:
        copy.wait_send()
    for list_ in (own, second, third, down):
        for condition, copies in list_:
            @pl.when(condition)
            def _():
                for copy in copies:
                    copy.wait_send()
    for i in range(CHUNKS):
        for copy in sends(i) + relays(i):
            copy.wait_send()
    for i in (0, 1):
        exchange(i).wait_send()


def attend_and_project(bounds, q, k, v, out_weight):
    vmem = pl.BlockSpec(memory_space=pltpu.VMEM)
    dma = pltpu.SemaphoreType.DMA
    return pl.pallas_call(
        main_kernel,
        out_shape=jax.ShapeDtypeStruct((HALF, 2048), bf16),
        in_specs=[vmem] + [pl.BlockSpec(memory_space=pl.ANY)] * 4,
        out_specs=vmem,
        scratch_shapes=[
            pltpu.VMEM((256, GROUP * BLOCK), bf16),
            pltpu.VMEM((SLOTS, BLOCK, 256), bf16),
            pltpu.VMEM((SLOTS, 128, BLOCK), bf16),
            pltpu.VMEM((CHUNKS, 1, TILE), f32),
            pltpu.VMEM((CHUNKS, 1, TILE), f32),
            pltpu.VMEM((CHUNKS, 128, TILE), f32),
            pltpu.VMEM((4, HALF, 2048), bf16),
            pltpu.VMEM((CHUNKS, 4, CHUNK, 512), bf16),
            pltpu.VMEM((2, CHUNK, 2048), f32),
            pltpu.VMEM((2, CHUNK, 2048), f32),
            pltpu.VMEM((BLOCK, TILE), f32),
            pltpu.VMEM((BLOCK, TILE), f32),
            dma((4,)), dma((3,)), dma((3,)),
            dma((11,)), dma((SLOTS,)), dma((11,)), dma((SLOTS,)),
            dma((2,)), dma((2,)), dma((3,)), dma((3,)), dma((3, 3)), dma((3, 3)),
            dma((CHUNKS, 4)), dma((CHUNKS, 4)), dma((2,)), dma((2,)),
        ],
        compiler_params=pltpu.CompilerParams(
            collective_id=0, has_side_effects=True, vmem_limit_bytes=60 * 2**20
        ),
    )(bounds, q, k, v, out_weight)


def per_device(queries, keys, values, lengths, out_weight):
    device = lax.axis_index("ctx")
    first = (device * HALF).astype(jnp.int32).reshape(1)
    q, k, v, bounds = prepare(lengths, first, queries, keys, values)
    return attend_and_project(bounds, q, k, v, out_weight)


def solution(mesh):
    return jax.shard_map(
        per_device,
        mesh=mesh,
        in_specs=(P("ctx", "head"), P("ctx", "head"), P("ctx", "head"), P(), P("head", None)),
        out_specs=P("ctx", "head"),
        check_vma=False,
    )
```

```python
import math

import jax
import jax.numpy as jnp
from jax import lax
from jax.experimental import pallas as pl
from jax.experimental.pallas import tpu as pltpu
from jax.sharding import PartitionSpec as P

f32, bf16 = jnp.float32, jnp.bfloat16
rope_base = 1000000.0
ramp_low = 23.0
ramp_high = 40.0
yarn_factor = 4.0
mscale = 0.1 * math.log(4.0) + 1.0
neg_large = -1e30
exp2_scale = math.log2(math.e) / math.sqrt(128.0)
doc_penalty = 131072.0

NDOCS = 8
BLOCK = 1024
GROUP = 4
HALF = 512
CHUNK = 256
TILE = GROUP * CHUNK
CHUNKS = BLOCK // CHUNK
SLOTS = 9
LAST = 4
MESH = pl.DeviceIdType.MESH


def inverse_frequencies():
    pair_index = jnp.arange(64).astype(f32)
    extrap = jnp.exp(-(2.0 * pair_index / 128.0) * math.log(rope_base))
    ramp = jnp.clip((pair_index - ramp_low) / (ramp_high - ramp_low), 0.0, 1.0)
    return extrap / yarn_factor * ramp + extrap * (1.0 - ramp)


def prepare_kernel(lengths, first_ref, inverse, queries, keys, values, q_ref, k_ref, v_ref, bounds_ref):
    first = first_ref[0] + pl.program_id(0) * CHUNK
    lane = lax.broadcasted_iota(jnp.int32, (CHUNK, 128), 1)
    at = first + lax.broadcasted_iota(jnp.int32, (CHUNK, 128), 0)
    start = jnp.zeros((CHUNK, 128), jnp.int32)
    document = lax.broadcasted_iota(jnp.int32, (128, CHUNK), 0)
    across = first + lax.broadcasted_iota(jnp.int32, (128, CHUNK), 1)
    hidden = document < NDOCS
    bound_row = lax.broadcasted_iota(jnp.int32, (8, 128), 0)
    bound_lane = lax.broadcasted_iota(jnp.int32, (8, 128), 1)
    bounds = jnp.zeros((8, 128), jnp.int32)
    end = 0
    for j in range(NDOCS):
        begin, end = end, end + lengths[j]
        start = start + jnp.where(at >= end, lengths[j], 0)
        hidden = hidden & ~((document == j) & (across >= begin) & (across < end))
        bounds = jnp.where((bound_lane == j) & (bound_row == 0), begin, bounds)
        bounds = jnp.where((bound_lane == j) & (bound_row == 1), end, bounds)
    bounds_ref[...] = bounds
    penalty = jnp.where(hidden, -doc_penalty, 0.0).astype(bf16)
    angles = (at - start).astype(f32) * inverse[...]
    cosine = jnp.cos(angles) * mscale
    sine = jnp.sin(angles) * mscale
    sine = jnp.where(lane < 64, -sine, sine)

    def rotated(ref, head):
        x = ref[:, head * 128 : (head + 1) * 128].astype(f32)
        return x * cosine + pltpu.roll(x, 64, 1) * sine

    for kv in range(2):
        for member in range(GROUP):
            cols = slice(member * CHUNK, (member + 1) * CHUNK)
            q_ref[kv, 0:128, cols] = jnp.transpose(rotated(queries, kv * GROUP + member)).astype(bf16)
            q_ref[kv, 128:256, cols] = penalty
        k_ref[kv] = rotated(keys, kv).astype(bf16)
        v_ref[kv] = jnp.transpose(values[:, kv * 128 : (kv + 1) * 128].astype(f32)).astype(bf16)


def prepare(lengths, first, queries, keys, values):
    inverse = inverse_frequencies()
    inverse = jnp.concatenate([inverse, inverse])[None, :]
    smem = pl.BlockSpec(memory_space=pltpu.SMEM)
    return pl.pallas_call(
        prepare_kernel,
        grid=(HALF // CHUNK,),
        out_shape=(
            jax.ShapeDtypeStruct((2, 256, GROUP * HALF), bf16),
            jax.ShapeDtypeStruct((2, HALF, 128), bf16),
            jax.ShapeDtypeStruct((2, 128, HALF), bf16),
            jax.ShapeDtypeStruct((8, 128), jnp.int32),
        ),
        in_specs=[
            smem,
            smem,
            pl.BlockSpec((1, 128), lambda i: (0, 0)),
            pl.BlockSpec((CHUNK, 1024), lambda i: (i, 0)),
            pl.BlockSpec((CHUNK, 256), lambda i: (i, 0)),
            pl.BlockSpec((CHUNK, 256), lambda i: (i, 0)),
        ],
        out_specs=(
            pl.BlockSpec((2, 256, TILE), lambda i: (0, 0, i)),
            pl.BlockSpec((2, CHUNK, 128), lambda i: (0, i, 0)),
            pl.BlockSpec((2, 128, CHUNK), lambda i: (0, 0, i)),
            pl.BlockSpec((8, 128), lambda i: (0, 0)),
        ),
        compiler_params=pltpu.CompilerParams(vmem_limit_bytes=62 * 2**20),
    )(lengths, first, inverse, queries, keys, values)


def main_kernel(
    bounds, qp, kp, vp, w_hbm, o_ref,
    q, kbuf, vbuf, top, total, acc, wbuf, att, given, taken, s_even, s_odd,
    local_sem, swap_send, swap_recv, k_send, k_recv, v_send, v_recv,
    w_send, w_recv, z_send, z_recv, c_send, c_recv, a_send, a_recv, p_send, p_recv,
):
    ctx = lax.axis_index("ctx")
    z = lax.axis_index("head")
    core = lax.rem(ctx, 2)
    chip = ctx // 2
    x = lax.rem(chip, 4)
    y = chip // 4
    other = 1 - core
    mate = (ctx + 1 - 2 * core, z)

    def at(x_, y_):
        return ((y_ * 4 + x_) * 2 + core, z)

    def remote(src, dst, send, recv, device):
        return pltpu.make_async_remote_copy(
            src_ref=src, dst_ref=dst, send_sem=send, recv_sem=recv, device_id=device, device_id_type=MESH
        )

    begin, end = bounds[0:1, :], bounds[1:2, :]

    def mark(slot):
        where = (chip - slot) * BLOCK + lax.broadcasted_iota(jnp.int32, (BLOCK, 128), 0)
        kbuf[slot, :, 128:256] = jnp.where((where >= begin) & (where < end), 1.0, 0.0).astype(bf16)

    barrier = pltpu.get_barrier_semaphore()
    pl.semaphore_signal(barrier, inc=1, device_id=mate, device_id_type=MESH)
    for step in (1, 2, 3):
        for device in (
            at(lax.rem(x + step, 4), y),
            at(x, lax.rem(y + step, 4)),
            (ctx, lax.rem(z + step, 4)),
        ):
            pl.semaphore_signal(barrier, inc=1, device_id=device, device_id_type=MESH)
    pl.semaphore_wait(barrier, 10)

    mine = pl.ds(pl.multiple_of(core * HALF, HALF), HALF)
    mine_q = pl.ds(pl.multiple_of(core * GROUP * HALF, GROUP * HALF), GROUP * HALF)
    swaps = [
        remote(kp.at[other], kbuf.at[0, mine, pl.ds(0, 128)], swap_send.at[0], swap_recv.at[0], mate),
        remote(vp.at[other], vbuf.at[0, :, mine], swap_send.at[1], swap_recv.at[1], mate),
        remote(qp.at[other], q.at[:, mine_q], swap_send.at[2], swap_recv.at[2], mate),
    ]
    for copy in swaps:
        copy.start()
    first_row = core * HALF

    def from_hbm(t, row, count):
        return w_hbm.at[
            pl.ds(pl.multiple_of(first_row + row, 64), count),
            pl.ds(pl.multiple_of(lax.rem(z + t, 4) * 2048, 2048), 2048),
        ]

    w_own = pltpu.make_async_copy(from_hbm(0, 0, HALF), wbuf.at[0], local_sem.at[3])
    w_whole = [
        remote(from_hbm(t, 0, 256), wbuf.at[t, pl.ds(0, 256), :], w_send.at[i], w_recv.at[i], (ctx, lax.rem(z + t, 4)))
        for i, t in enumerate((1, 3))
    ]

    def piece_of(t, which):
        size, base = (128, 0) if t == 2 else (64, 256)
        return pl.ds(pl.multiple_of(base + which * size, 64), size)

    def own_piece(t):
        return y if t == 2 else x

    w_pieces, w_spread, w_awaited = [], [], []
    for i, t in enumerate((2, 1, 3)):
        size, base = (128, 0) if t == 2 else (64, 256)
        held = wbuf.at[t, piece_of(t, own_piece(t)), :]
        w_pieces.append(
            remote(
                from_hbm(t, base + own_piece(t) * size, size), held,
                z_send.at[i], z_recv.at[i], (ctx, lax.rem(z + t, 4)),
            )
        )
        for step in (1, 2, 3) if t != 2 else ():
            to = lax.rem(own_piece(t) + step, 4)
            device = at(to, y)
            w_spread.append(remote(held, held, c_send.at[i, step - 1], c_recv.at[i, step - 1], device))
            came = lax.rem(own_piece(t) + 4 - step, 4)
            w_awaited.append(
                remote(held, wbuf.at[t, piece_of(t, came), :], c_send.at[i, step - 1], c_recv.at[i, step - 1], mate)
            )

    def spread_weights():
        for copy in w_pieces[1:]:
            copy.wait_recv()
        for copy in w_spread:
            copy.start()

    def down_y(k):
        held = wbuf.at[2, piece_of(2, lax.rem(y + k, 4)), :]
        return remote(held, held, c_send.at[0, k], c_recv.at[0, k], at(x, lax.rem(y + 3, 4)))

    def from_up_y(k):
        held = wbuf.at[2, piece_of(2, lax.rem(y + k + 1, 4)), :]
        return remote(held, held, c_send.at[0, k], c_recv.at[0, k], mate)

    def hand_on(k):
        (from_up_y(k - 1) if k else w_pieces[0]).wait_recv()
        down_y(k).start()

    locals_ = [
        pltpu.make_async_copy(kp.at[core], kbuf.at[0, mine, pl.ds(0, 128)], local_sem.at[0]),
        pltpu.make_async_copy(vp.at[core], vbuf.at[0, :, mine], local_sem.at[1]),
        pltpu.make_async_copy(qp.at[core], q.at[:, mine_q], local_sem.at[2]),
    ]
    for copy in locals_:
        copy.start()
    for copy in w_pieces + w_whole:
        copy.start()
    w_own.start()
    mark(0)

    def share(slot, far, device, index):
        return (
            remote(kbuf.at[slot, :, pl.ds(0, 128)], kbuf.at[far, :, pl.ds(0, 128)], k_send.at[index], k_recv.at[far], device),
            remote(vbuf.at[slot], vbuf.at[far], v_send.at[index], v_recv.at[far], device),
        )

    below = at(x, lax.rem(y + 1, 4))
    own = [(y <= 2, share(0, 4, below, 0))]
    second = [((y >= 1) & (y <= 2), share(4, 8, below, 1))]
    third = []
    for step in (1, 3, 2):
        x_ = lax.rem(x + step, 4)
        near = step != 2
        own.append((x_ > x, share(0, lax.rem(4 + x_ - x, 4), at(x_, y), 1 + step)))
        second.append((y >= 1 if near else (y >= 1) & (x_ < x), share(4, 4 + x_ - x, at(x_, y), 4 + step)))
        if near:
            third.append(((y >= 2) & (x_ < x), share(8, lax.rem(8 + x_ - x, 9), at(x_, y), 7 + step)))
    down = [((y <= 2) & (chip >= 2), share(2, 6, below, 9))]

    def pass_on(list_, slot=None, rows_before=0):
        for part in (0, 1):
            if slot is not None:
                @pl.when(y >= rows_before)
                def _():
                    share(slot, slot, mate, 0)[part].wait_recv()
            for condition, copies in list_:
                @pl.when(condition)
                def _():
                    copies[part].start()

    def arrived(slot):
        @pl.when((slot != 4) & (slot != 8))
        def _():
            for copy in share(slot, slot, mate, 0):
                copy.wait_recv()

        @pl.when(slot == 2)
        def _():
            pass_on(down)

        @pl.when(slot == 8)
        def _():
            pass_on(third, 8, 2)

    for copy in swaps[:2]:
        copy.wait_recv()
    for copy in locals_[:2]:
        copy.wait()
    pass_on(own)
    for slot in range(1, SLOTS):
        mark(slot)
    swaps[2].wait_recv()
    locals_[2].wait()

    for chunk in range(CHUNKS):
        cols = slice(chunk * TILE, (chunk + 1) * TILE)
        seen = (chunk + 1) * CHUNK
        s = jnp.dot(kbuf[0, 0:seen, :], q[:, cols], preferred_element_type=f32)
        key = lax.broadcasted_iota(jnp.int32, s.shape, 0)
        query = chunk * CHUNK + lax.rem(lax.broadcasted_iota(jnp.int32, s.shape, 1), CHUNK)
        s = jnp.where(key <= query, s, neg_large)
        new = jnp.max(s, axis=0, keepdims=True)
        p = jnp.exp2((s - new) * exp2_scale)
        top[chunk] = new
        total[chunk] = jnp.sum(p, axis=0, keepdims=True)
        acc[chunk] = jnp.dot(vbuf[0, :, 0:seen], p.astype(bf16), preferred_element_type=f32)

    def scores(slot, chunk):
        cols = pl.ds(pl.multiple_of(chunk * TILE, TILE), TILE)
        return jnp.dot(kbuf[slot], q[:, cols], preferred_element_type=f32)

    def add(scores_ref, slot, chunk):
        s = scores_ref[...]
        old = top[chunk]
        new = jnp.maximum(old, jnp.max(s, axis=0, keepdims=True))
        p = jnp.exp2((s - new) * exp2_scale)
        scale = jnp.exp2((old - new) * exp2_scale)
        total[chunk] = total[chunk] * scale + jnp.sum(p, axis=0, keepdims=True)
        top[chunk] = new
        acc[chunk] = acc[chunk] * scale + jnp.dot(vbuf[slot], p.astype(bf16), preferred_element_type=f32)

    def slot_of(i):
        shift = jnp.where(y >= 2, 1, 0)
        j = i - shift
        of_second = jnp.where(j < 4, j, j + 1)
        rest = jnp.where(j <= x + 3, of_second, i)
        column = jnp.where(i == x, 4, jnp.where((y >= 2) & (i == x + 1), 8, rest))
        return jnp.where(i < x, i + 1, column)

    def chunk_of(i):
        return lax.rem(i + 2 * other, CHUNKS)

    def sends(i):
        return [
            remote(att.at[i, 0], att.at[i, t], a_send.at[i, t], a_recv.at[i, t], (ctx, lax.rem(z + t, 4)))
            for t in (1, 3)
        ]

    def relays(i):
        copies = []
        for t, half, index in ((1, 0, 0), (3, 1, 2)):
            part = pl.ds(half * (CHUNK // 2), CHUNK // 2)
            copies.append(
                remote(
                    att.at[i, t, part, :], att.at[i, 2, part, :],
                    a_send.at[i, index], a_recv.at[i, index], (ctx, lax.rem(z + t, 4)),
                )
            )
        return copies

    def relay(i):
        for copy in sends(i):
            copy.wait_recv()
        for copy in relays(i):
            copy.start()

    def finish(i):
        chunk = chunk_of(i)
        out = acc[chunk] / total[chunk]
        for member in range(GROUP):
            cols = slice(member * CHUNK, (member + 1) * CHUNK)
            att[i, 0, :, member * 128 : (member + 1) * 128] = jnp.transpose(out[:, cols]).astype(bf16)
        for copy in sends(i):
            copy.start()

    pass_on(second, 4, 1)
    hand_on(0)
    blocks = jnp.minimum(8, chip)

    @pl.when(blocks >= LAST)
    def _():
        arrived(slot_of(0))
        s_even[...] = scores(slot_of(0), jnp.where(blocks > LAST, 0, chunk_of(0)))

        def block_step(i, _):
            slot, later = slot_of(i), slot_of(i + 1)

            s_odd[...] = scores(slot, 1)
            add(s_even, slot, 0)
            s_even[...] = scores(slot, 2)
            add(s_odd, slot, 1)
            arrived(later)
            s_odd[...] = scores(slot, 3)
            add(s_even, slot, 2)
            s_even[...] = scores(later, jnp.where(i + 1 < blocks - LAST, 0, chunk_of(0)))
            add(s_odd, slot, 3)
            return 0

        lax.fori_loop(0, blocks - LAST, block_step, 0)

        def chunk_step(i, _):
            chunk = chunk_of(i)
            slots = [slot_of(blocks - LAST + j) for j in range(LAST)]

            @pl.when(i == 0)
            def _():
                hand_on(1)
                spread_weights()

            @pl.when(i == 1)
            def _():
                hand_on(2)

            @pl.when(i >= 2)
            def _():
                relay(i - 2)

            for j in range(LAST):
                ready, coming = (s_even, s_odd) if j % 2 == 0 else (s_odd, s_even)
                if j + 1 < LAST:
                    @pl.when(i == 0)
                    def _():
                        arrived(slots[j + 1])

                    coming[...] = scores(slots[j + 1], chunk)
                else:
                    coming[...] = scores(slots[0], chunk_of(i + 1))
                add(ready, slots[j], chunk)
            finish(i)
            return 0

        lax.fori_loop(0, CHUNKS, chunk_step, 0)

    @pl.when(blocks < LAST)
    def _():
        def block_here(j, _):
            arrived(slot_of(j))
            return 0

        lax.fori_loop(0, blocks, block_here, 0)

        def chunk_step(i, _):
            def one(j, _):
                s_even[...] = scores(slot_of(j), chunk_of(i))
                add(s_even, slot_of(j), chunk_of(i))
                return 0

            @pl.when(i == 0)
            def _():
                hand_on(1)
                spread_weights()

            @pl.when(i == 1)
            def _():
                hand_on(2)

            @pl.when(i >= 2)
            def _():
                relay(i - 2)

            lax.fori_loop(0, blocks, one, 0)
            finish(i)
            return 0

        lax.fori_loop(0, CHUNKS, chunk_step, 0)

    relay(2)
    w_own.wait()
    for copy in w_whole:
        copy.wait_recv()
    for copy in w_awaited + [from_up_y(2)]:
        copy.wait_recv()

    def exchange(i):
        return remote(given.at[i], taken.at[i], p_send.at[i], p_recv.at[i], mate)

    def project(i, keep):
        for copy in relays(i):
            copy.wait_recv()

        def some(n, _):
            cols = pl.ds(pl.multiple_of(n * 512, 512), 512)
            part = jnp.dot(att[i, 0], wbuf[0, :, cols], preferred_element_type=f32)
            for s in (1, 2, 3):
                part = part + jnp.dot(att[i, s], wbuf[s, :, cols], preferred_element_type=f32)
            keep(cols, part)
            return 0

        lax.fori_loop(0, 4, some, 0)

    for i in (0, 1):
        def give(cols, part):
            given[i, :, cols] = part

        project(i, give)
        exchange(i).start()
        if i == 0:
            relay(3)
    for i in (0, 1):
        exchange(i).wait_recv()

        def keep(cols, part):
            o_ref[i * CHUNK : (i + 1) * CHUNK, cols] = (part + taken[i, :, cols]).astype(bf16)

        project(i + 2, keep)

    for copy in swaps + w_whole + w_pieces + w_spread + [down_y(k) for k in range(3)]:
        copy.wait_send()
    for list_ in (own, second, third, down):
        for condition, copies in list_:
            @pl.when(condition)
            def _():
                for copy in copies:
                    copy.wait_send()
    for i in range(CHUNKS):
        for copy in sends(i) + relays(i):
            copy.wait_send()
    for i in (0, 1):
        exchange(i).wait_send()


def attend_and_project(bounds, q, k, v, out_weight):
    vmem = pl.BlockSpec(memory_space=pltpu.VMEM)
    dma = pltpu.SemaphoreType.DMA
    return pl.pallas_call(
        main_kernel,
        out_shape=jax.ShapeDtypeStruct((HALF, 2048), bf16),
        in_specs=[vmem] + [pl.BlockSpec(memory_space=pl.ANY)] * 4,
        out_specs=vmem,
        scratch_shapes=[
            pltpu.VMEM((256, GROUP * BLOCK), bf16),
            pltpu.VMEM((SLOTS, BLOCK, 256), bf16),
            pltpu.VMEM((SLOTS, 128, BLOCK), bf16),
            pltpu.VMEM((CHUNKS, 1, TILE), f32),
            pltpu.VMEM((CHUNKS, 1, TILE), f32),
            pltpu.VMEM((CHUNKS, 128, TILE), f32),
            pltpu.VMEM((4, HALF, 2048), bf16),
            pltpu.VMEM((CHUNKS, 4, CHUNK, 512), bf16),
            pltpu.VMEM((2, CHUNK, 2048), f32),
            pltpu.VMEM((2, CHUNK, 2048), f32),
            pltpu.VMEM((BLOCK, TILE), f32),
            pltpu.VMEM((BLOCK, TILE), f32),
            dma((4,)), dma((3,)), dma((3,)),
            dma((11,)), dma((SLOTS,)), dma((11,)), dma((SLOTS,)),
            dma((2,)), dma((2,)), dma((3,)), dma((3,)), dma((3, 3)), dma((3, 3)),
            dma((CHUNKS, 4)), dma((CHUNKS, 4)), dma((2,)), dma((2,)),
        ],
        compiler_params=pltpu.CompilerParams(
            collective_id=0, has_side_effects=True, vmem_limit_bytes=60 * 2**20
        ),
    )(bounds, q, k, v, out_weight)


def per_device(queries, keys, values, lengths, out_weight):
    device = lax.axis_index("ctx")
    first = (device * HALF).astype(jnp.int32).reshape(1)
    q, k, v, bounds = prepare(lengths, first, queries, keys, values)
    return attend_and_project(bounds, q, k, v, out_weight)


def solution(mesh):
    return jax.shard_map(
        per_device,
        mesh=mesh,
        in_specs=(P("ctx", "head"), P("ctx", "head"), P("ctx", "head"), P(), P("head", None)),
        out_specs=P("ctx", "head"),
        check_vma=False,
    )
```
